32 devices in a mesh: tok: 8 (over z, y), feat: 4 (over x, core).
Axes of the slice: x: 2, y: 2, z: 4, core: 2. Of those that a mesh axis runs over, the one named last changes fastest.
Arguments:
- inputs: bfloat16 [4096, 960], P('tok', 'feat'), may hold values from -6 to 6
- attn_gain: float32 [960], P('feat'), may hold values from 0.5 to 1.5
- w_query: bfloat16 [960, 960], P('feat', 'tok'), may hold values from -0.1875 to 0.1875
- w_key: bfloat16 [960, 320], P('feat', 'tok'), may hold values from -0.1875 to 0.1875
- value_weight: bfloat16 [960, 320], P('feat', 'tok'), may hold values from -0.1875 to 0.1875
- w_out: bfloat16 [960, 960], P('tok', 'feat'), may hold values from -1 to 1
- ffn_gain: float32 [960], P('feat'), may hold values from 0.5 to 1.5
- w_gate: bfloat16 [960, 2560], P('tok', 'feat'), may hold values from -0.1875 to 0.1875
- w_up: bfloat16 [960, 2560], P('tok', 'feat'), may hold values from -0.1875 to 0.1875
- w_down: bfloat16 [2560, 960], P('feat', 'tok'), may hold values from -0.125 to 0.125
- cot: bfloat16 [4096, 960], P('tok', 'feat'), may hold values from -6 to 6
Outputs:
- block_out: float32 [960, 4096], P('feat', 'tok')
- grad_inputs: float32 [960, 4096], P('feat', 'tok')
- grad_attn_gain: float32 [960], P('feat')
- grad_w_query: float32 [960, 960], P('feat', 'tok')
- grad_w_key: float32 [960, 320], P('feat', 'tok')
- grad_w_value: float32 [960, 320], P('feat', 'tok')
- grad_w_out: float32 [960, 960], P('tok', 'feat')
- grad_ffn_gain: float32 [960], P('feat')
- grad_w_gate: float32 [960, 2560], P('tok', 'feat')
- grad_w_up: float32 [960, 2560], P('tok', 'feat')
- grad_w_down: float32 [2560, 960], P('feat', 'tok')
The draws below stay inside these ranges and needn't reach their ends.
All inputs are finite; a program needn't handle non-finite values.
Results may differ from the reference program's by a relative error of at most 0.02.
Values may be sent and summed in bfloat16 or wider, within the bound.
A program may use at most 128 MiB of HBM per device.

```python
import math
import jax
import jax.numpy as jnp
from jax import lax

MODEL_WIDTH = 960
QUERY_HEADS = 15
KEY_HEADS = 5
HEAD_SIZE = 64
FF = 2560
SEQ_LEN = 4096
QUERY_PER_KEY = 3
TOKEN_TOTAL = 4096


def levels(own_key, shape, split, least, top_value):
    level, own = 1.0, jax.random.fold_in(own_key, 6)
    for axis_at, shards_of in split:
        heights = jnp.exp(jax.random.uniform(jax.random.fold_in(own, axis_at), (shards_of,), jnp.float32, least / len(split), top_value / len(split)))
        level = level * jnp.repeat(heights, shape[axis_at] // shards_of).reshape([-1 if axis == axis_at else 1 for axis in range(len(shape))])
    return level


def centred(key, dims, deviation, limit, shards=(), held_as=jnp.bfloat16):
    result = deviation * jax.random.normal(key, dims, jnp.float32)
    if shards:
        result = result * levels(key, dims, shards, -0.22, 0.18)
    return jnp.clip(result, -limit, limit).astype(held_as)


def setup_inputs(seed: int = 0) -> dict:
    key_of = jax.random.split(jax.random.key(seed), 12)
    inputs = centred(key_of[0], (TOKEN_TOTAL, MODEL_WIDTH), 1.0, 6.0, ((0, 8), (1, 4)))
    attn_gain = jnp.clip(1.0 + 0.1 * jax.random.normal(key_of[1], (MODEL_WIDTH,), jnp.float32), 0.5, 1.5)
    w_query = centred(key_of[2], (MODEL_WIDTH, QUERY_HEADS * HEAD_SIZE), MODEL_WIDTH ** -0.5, 0.1875, ((0, 4), (1, 8)))
    w_key = centred(key_of[3], (MODEL_WIDTH, KEY_HEADS * HEAD_SIZE), MODEL_WIDTH ** -0.5, 0.1875, ((0, 4), (1, 8)))
    value_weight = centred(key_of[4], (MODEL_WIDTH, KEY_HEADS * HEAD_SIZE), MODEL_WIDTH ** -0.5, 0.1875, ((0, 4), (1, 8)))
    w_out = centred(key_of[5], (QUERY_HEADS * HEAD_SIZE, MODEL_WIDTH), (QUERY_HEADS * HEAD_SIZE // 32) ** -0.5, 1.0, ((0, 8), (1, 4)))
    ffn_gain = jnp.clip(1.0 + 0.1 * jax.random.normal(key_of[6], (MODEL_WIDTH,), jnp.float32), 0.5, 1.5)
    w_gate = centred(key_of[7], (MODEL_WIDTH, FF), MODEL_WIDTH ** -0.5, 0.1875, ((0, 8), (1, 4)))
    w_up = centred(key_of[8], (MODEL_WIDTH, FF), MODEL_WIDTH ** -0.5, 0.1875, ((0, 8), (1, 4)))
    w_down = centred(key_of[9], (FF, MODEL_WIDTH), FF ** -0.5, 0.125, ((0, 4), (1, 8)))
    cot = centred(key_of[10], (TOKEN_TOTAL, MODEL_WIDTH), 1.0, 6.0, ((0, 8), (1, 4)))
    return dict(inputs=inputs, attn_gain=attn_gain, w_query=w_query, w_key=w_key, value_weight=value_weight, w_out=w_out, ffn_gain=ffn_gain, w_gate=w_gate, w_up=w_up, w_down=w_down, cot=cot)


EPS = 1e-05
ROPE_BASE = 10000.0
LARGE_NEGATIVE = -1e+30

def rotary_tables(positions):
    half_width = HEAD_SIZE // 2
    inverse_freq = ROPE_BASE ** (-2.0 * jnp.arange(half_width, dtype=jnp.float32) / HEAD_SIZE)
    angles = positions.astype(jnp.float32)[:, None] * inverse_freq[None, :]
    return (jnp.cos(angles)[:, None, :], jnp.sin(angles)[:, None, :])

def apply_rotary(value_matrix, cosine_lookup, sine_lookup, head_count, sign_value):
    shaped = value_matrix.reshape(value_matrix.shape[0], head_count, HEAD_SIZE)
    lead_half = shaped[..., :HEAD_SIZE // 2]
    tail_half = shaped[..., HEAD_SIZE // 2:]
    out_lead = lead_half * cosine_lookup - sign_value * tail_half * sine_lookup
    out_tail = tail_half * cosine_lookup + sign_value * lead_half * sine_lookup
    return jnp.concatenate([out_lead, out_tail], axis=-1).reshape(value_matrix.shape[0], head_count * HEAD_SIZE)

def divide_pair(value_matrix):
    high = value_matrix.astype(jnp.bfloat16)
    high = lax.optimization_barrier(high)
    low = (value_matrix - high.astype(jnp.float32)).astype(jnp.bfloat16)
    return high.astype(jnp.float32) + low.astype(jnp.float32)

def attend_forward(query_matrix, key_matrix, value_matrix):
    rows_per_block = min(512, SEQ_LEN)
    n_blocks = TOKEN_TOTAL // rows_per_block
    score_scale = 1.0 / math.sqrt(HEAD_SIZE)

    def one_block(block_number):
        query_tile = lax.dynamic_slice_in_dim(query_matrix, (block_number * rows_per_block).astype(jnp.int32), rows_per_block, 0)
        query_tile = query_tile.astype(jnp.float32).reshape(rows_per_block, KEY_HEADS, QUERY_PER_KEY, HEAD_SIZE)
        q_pos = block_number * rows_per_block + jnp.arange(rows_per_block, dtype=jnp.int32)
        first_key_block = block_number * rows_per_block // SEQ_LEN * (SEQ_LEN // rows_per_block)

        def step_forward(key_block_rows, carried):
            maxima, totals, weighted = carried
            key_tile = lax.dynamic_slice_in_dim(key_matrix, (key_block_rows * rows_per_block).astype(jnp.int32), rows_per_block, 0)
            value_tile = lax.dynamic_slice_in_dim(value_matrix, (key_block_rows * rows_per_block).astype(jnp.int32), rows_per_block, 0)
            key_tile = key_tile.astype(jnp.float32).reshape(rows_per_block, KEY_HEADS, HEAD_SIZE)
            value_tile = value_tile.astype(jnp.float32).reshape(rows_per_block, KEY_HEADS, HEAD_SIZE)
            scores = jnp.einsum('rgcd,ngd->gcrn', query_tile, key_tile) * score_scale
            k_pos = key_block_rows * rows_per_block + jnp.arange(rows_per_block, dtype=jnp.int32)
            allowed = k_pos[None, :] <= q_pos[:, None]
            masked = jnp.where(allowed, scores, LARGE_NEGATIVE)
            new_max = jnp.maximum(maxima, lax.optimization_barrier(jnp.max(masked, axis=-1)))
            weights = jnp.where(allowed, jnp.exp(masked - new_max[..., None]), 0.0)
            factor = jnp.exp(maxima - new_max)
            totals = totals * factor + lax.optimization_barrier(jnp.sum(weights, axis=-1))
            weighted = weighted * factor[..., None] + jnp.einsum('gcrn,ngd->gcrd', weights, value_tile)
            return (new_max, totals, weighted)
        starting_state = (jnp.full((KEY_HEADS, QUERY_PER_KEY, rows_per_block), LARGE_NEGATIVE, jnp.float32), jnp.zeros((KEY_HEADS, QUERY_PER_KEY, rows_per_block), jnp.float32), jnp.zeros((KEY_HEADS, QUERY_PER_KEY, rows_per_block, HEAD_SIZE), jnp.float32))
        maxima, totals, weighted = lax.fori_loop(first_key_block.astype(jnp.int32), (block_number + 1).astype(jnp.int32), step_forward, starting_state)
        heads = (weighted / totals[..., None]).transpose(2, 0, 1, 3).reshape(rows_per_block, QUERY_HEADS * HEAD_SIZE)
        logsumexp_totals = (maxima + jnp.log(totals)).transpose(2, 0, 1).reshape(rows_per_block, QUERY_HEADS)
        return (heads, logsumexp_totals)
    heads, logsumexp_totals = lax.map(one_block, jnp.arange(n_blocks, dtype=jnp.int32))
    return (heads.reshape(TOKEN_TOTAL, QUERY_HEADS * HEAD_SIZE), logsumexp_totals.reshape(TOKEN_TOTAL, QUERY_HEADS))

def attend_backward(query_matrix, key_matrix, value_matrix, head_gradient, logsumexp_taken, difference_taken):
    rows_per_block = min(512, SEQ_LEN)
    n_blocks = TOKEN_TOTAL // rows_per_block
    score_scale = 1.0 / math.sqrt(HEAD_SIZE)

    def query_side(block_number):
        start_position = (block_number * rows_per_block).astype(jnp.int32)
        return (lax.dynamic_slice_in_dim(query_matrix, start_position, rows_per_block, 0).astype(jnp.float32).reshape(rows_per_block, KEY_HEADS, QUERY_PER_KEY, HEAD_SIZE), lax.dynamic_slice_in_dim(head_gradient, start_position, rows_per_block, 0).astype(jnp.float32).reshape(rows_per_block, KEY_HEADS, QUERY_PER_KEY, HEAD_SIZE), lax.dynamic_slice_in_dim(logsumexp_taken, start_position, rows_per_block, 0).reshape(rows_per_block, KEY_HEADS, QUERY_PER_KEY).transpose(1, 2, 0), lax.dynamic_slice_in_dim(difference_taken, start_position, rows_per_block, 0).reshape(rows_per_block, KEY_HEADS, QUERY_PER_KEY).transpose(1, 2, 0), block_number * rows_per_block + jnp.arange(rows_per_block, dtype=jnp.int32))

    def key_side(key_block_rows):
        start_position = (key_block_rows * rows_per_block).astype(jnp.int32)
        return (lax.dynamic_slice_in_dim(key_matrix, start_position, rows_per_block, 0).astype(jnp.float32).reshape(rows_per_block, KEY_HEADS, HEAD_SIZE), lax.dynamic_slice_in_dim(value_matrix, start_position, rows_per_block, 0).astype(jnp.float32).reshape(rows_per_block, KEY_HEADS, HEAD_SIZE), key_block_rows * rows_per_block + jnp.arange(rows_per_block, dtype=jnp.int32))

    def pair_terms(query_block, key_block_rows):
        query_tile, do_block, lse_block, delta_block, q_pos = query_side(query_block)
        key_tile, value_tile, k_pos = key_side(key_block_rows)
        scores = jnp.einsum('rgcd,ngd->gcrn', query_tile, key_tile) * score_scale
        allowed = k_pos[None, :] <= q_pos[:, None]
        masked = jnp.where(allowed, scores, LARGE_NEGATIVE)
        probability = jnp.where(allowed, jnp.exp(masked - lse_block[..., None]), 0.0)
        d_probs = jnp.einsum('rgcd,ngd->gcrn', do_block, value_tile)
        d_scores = probability * (d_probs - delta_block[..., None])
        return (probability, d_scores, query_tile, do_block, key_tile)

    def one_query_block(block_number):
        first_key_block = block_number * rows_per_block // SEQ_LEN * (SEQ_LEN // rows_per_block)

        def step_forward(key_block_rows, query_gradient_sum):
            probability, d_scores, query_tile, do_block, key_tile = pair_terms(block_number, key_block_rows)
            return query_gradient_sum + jnp.einsum('gcrn,ngd->gcrd', d_scores, key_tile) * score_scale
        query_gradient_sum = lax.fori_loop(first_key_block.astype(jnp.int32), (block_number + 1).astype(jnp.int32), step_forward, jnp.zeros((KEY_HEADS, QUERY_PER_KEY, rows_per_block, HEAD_SIZE), jnp.float32))
        return query_gradient_sum.transpose(2, 0, 1, 3).reshape(rows_per_block, QUERY_HEADS * HEAD_SIZE)

    def one_key_block(key_block_rows):
        last_qb = (key_block_rows * rows_per_block // SEQ_LEN + 1) * (SEQ_LEN // rows_per_block)

        def step_forward(query_block, sums):
            key_gradient_sum, value_gradient_sum = sums
            probability, d_scores, query_tile, do_block, key_tile = pair_terms(query_block, key_block_rows)
            value_gradient_sum = value_gradient_sum + jnp.einsum('gcrn,rgcd->ngd', probability, do_block)
            key_gradient_sum = key_gradient_sum + jnp.einsum('gcrn,rgcd->ngd', d_scores, query_tile) * score_scale
            return (key_gradient_sum, value_gradient_sum)
        starting_state = (jnp.zeros((rows_per_block, KEY_HEADS, HEAD_SIZE), jnp.float32), jnp.zeros((rows_per_block, KEY_HEADS, HEAD_SIZE), jnp.float32))
        key_gradient_sum, value_gradient_sum = lax.fori_loop(key_block_rows.astype(jnp.int32), last_qb.astype(jnp.int32), step_forward, starting_state)
        return (key_gradient_sum.reshape(rows_per_block, KEY_HEADS * HEAD_SIZE), value_gradient_sum.reshape(rows_per_block, KEY_HEADS * HEAD_SIZE))
    queries_gradient = lax.map(one_query_block, jnp.arange(n_blocks, dtype=jnp.int32)).reshape(TOKEN_TOTAL, QUERY_HEADS * HEAD_SIZE)
    keys_gradient, values_gradient = lax.map(one_key_block, jnp.arange(n_blocks, dtype=jnp.int32))
    return (queries_gradient, keys_gradient.reshape(TOKEN_TOTAL, KEY_HEADS * HEAD_SIZE), values_gradient.reshape(TOKEN_TOTAL, KEY_HEADS * HEAD_SIZE))

def reference(inputs, attn_gain, w_query, w_key, value_weight, w_out, ffn_gain, w_gate, w_up, w_down, cot):
    inputs_wide = inputs.astype(jnp.float32)
    scale_one = lax.rsqrt(lax.optimization_barrier(jnp.mean(inputs_wide * inputs_wide, axis=1, keepdims=True)) + EPS)
    normed_one = (inputs_wide * scale_one * attn_gain[None, :]).astype(jnp.bfloat16)
    query_pre = jnp.dot(normed_one, w_query, preferred_element_type=jnp.float32)
    key_unrotated = jnp.dot(normed_one, w_key, preferred_element_type=jnp.float32)
    value_pre = jnp.dot(normed_one, value_weight, preferred_element_type=jnp.float32)
    positions = jnp.arange(TOKEN_TOTAL, dtype=jnp.int32) % SEQ_LEN
    cosine_lookup, sine_lookup = rotary_tables(positions)
    query_matrix = apply_rotary(query_pre, cosine_lookup, sine_lookup, QUERY_HEADS, 1.0).astype(jnp.bfloat16)
    key_matrix = apply_rotary(key_unrotated, cosine_lookup, sine_lookup, KEY_HEADS, 1.0).astype(jnp.bfloat16)
    value_matrix = value_pre.astype(jnp.bfloat16)
    heads_wide, logsumexp_totals = attend_forward(query_matrix, key_matrix, value_matrix)
    heads_out = heads_wide.astype(jnp.bfloat16)
    residual = inputs_wide + jnp.dot(heads_out, w_out, preferred_element_type=jnp.float32)
    scale_two = lax.rsqrt(lax.optimization_barrier(jnp.mean(residual * residual, axis=1, keepdims=True)) + EPS)
    normed_two = (residual * scale_two * ffn_gain[None, :]).astype(jnp.bfloat16)
    gate_pre = jnp.dot(normed_two, w_gate, preferred_element_type=jnp.float32)
    up_pre = jnp.dot(normed_two, w_up, preferred_element_type=jnp.float32)
    sigmoid_gate = jax.nn.sigmoid(gate_pre)
    hidden = (gate_pre * sigmoid_gate * up_pre).astype(jnp.bfloat16)
    block_out = residual + jnp.dot(hidden, w_down, preferred_element_type=jnp.float32)
    cot_wide = cot.astype(jnp.float32)
    grad_w_down = jnp.dot(hidden.T, cot, preferred_element_type=jnp.float32)
    d_hidden = jnp.dot(cot, w_down.T, preferred_element_type=jnp.float32)
    d_gate = (d_hidden * up_pre * sigmoid_gate * (1.0 + gate_pre * (1.0 - sigmoid_gate))).astype(jnp.bfloat16)
    d_up = (d_hidden * gate_pre * sigmoid_gate).astype(jnp.bfloat16)
    grad_w_gate = jnp.dot(normed_two.T, d_gate, preferred_element_type=jnp.float32)
    grad_w_up = jnp.dot(normed_two.T, d_up, preferred_element_type=jnp.float32)
    d_normed_two = jnp.dot(d_gate, w_gate.T, preferred_element_type=jnp.float32) + jnp.dot(d_up, w_up.T, preferred_element_type=jnp.float32)
    stat_two = lax.optimization_barrier(jnp.sum(d_normed_two * ffn_gain[None, :] * residual, axis=1, keepdims=True))
    d_mid = cot_wide + scale_two * ffn_gain[None, :] * d_normed_two - residual * scale_two ** 3 * stat_two / MODEL_WIDTH
    grad_ffn_gain = lax.optimization_barrier(jnp.sum(d_normed_two * residual * scale_two, axis=0))
    d_attn = d_mid.astype(jnp.bfloat16)
    grad_w_out = jnp.dot(heads_out.T, d_attn, preferred_element_type=jnp.float32)
    head_gradient = jnp.dot(d_attn, w_out.T, preferred_element_type=jnp.float32).astype(jnp.bfloat16)
    delta = lax.optimization_barrier(jnp.sum((head_gradient.astype(jnp.float32) * heads_out.astype(jnp.float32)).reshape(TOKEN_TOTAL, QUERY_HEADS, HEAD_SIZE), axis=-1))
    logsumexp_taken = divide_pair(logsumexp_totals)
    difference_taken = divide_pair(delta)
    queries_gradient, keys_gradient, values_gradient = attend_backward(query_matrix, key_matrix, value_matrix, head_gradient, logsumexp_taken, difference_taken)
    d_query = apply_rotary(queries_gradient, cosine_lookup, sine_lookup, QUERY_HEADS, -1.0).astype(jnp.bfloat16)
    key_gradient = apply_rotary(keys_gradient, cosine_lookup, sine_lookup, KEY_HEADS, -1.0).astype(jnp.bfloat16)
    d_value = values_gradient.astype(jnp.bfloat16)
    grad_w_query = jnp.dot(normed_one.T, d_query, preferred_element_type=jnp.float32)
    grad_w_key = jnp.dot(normed_one.T, key_gradient, preferred_element_type=jnp.float32)
    grad_w_value = jnp.dot(normed_one.T, d_value, preferred_element_type=jnp.float32)
    d_normed_one = jnp.dot(d_query, w_query.T, preferred_element_type=jnp.float32) + jnp.dot(key_gradient, w_key.T, preferred_element_type=jnp.float32) + jnp.dot(d_value, value_weight.T, preferred_element_type=jnp.float32)
    stat_one = lax.optimization_barrier(jnp.sum(d_normed_one * attn_gain[None, :] * inputs_wide, axis=1, keepdims=True))
    grad_inputs = d_mid + scale_one * attn_gain[None, :] * d_normed_one - inputs_wide * scale_one ** 3 * stat_one / MODEL_WIDTH
    grad_attn_gain = lax.optimization_barrier(jnp.sum(d_normed_one * inputs_wide * scale_one, axis=0))
    return (block_out.T, grad_inputs.T, grad_attn_gain, grad_w_query, grad_w_key, grad_w_value, grad_w_out, grad_ffn_gain, grad_w_gate, grad_w_up, grad_w_down)
```

```python
import itertools
import math

import jax
import jax.numpy as jnp
from jax import lax
from jax.experimental import pallas as pl
from jax.experimental.pallas import tpu as pltpu
from jax.sharding import PartitionSpec as P

MODEL_WIDTH = 960
QUERY_HEADS = 15
KEY_HEADS = 5
HEAD_SIZE = 64
SEQ_LEN = 4096
QUERY_PER_KEY = 3


EPS = 1e-05
ROPE_BASE = 10000.0
LARGE_NEGATIVE = -1e30


def rotary_tables(positions):
    half_width = HEAD_SIZE // 2
    inverse_freq = ROPE_BASE ** (-2.0 * jnp.arange(half_width, dtype=jnp.float32) / HEAD_SIZE)
    angles = positions.astype(jnp.float32)[:, None] * inverse_freq[None, :]
    return (jnp.cos(angles)[:, None, :], jnp.sin(angles)[:, None, :])


def apply_rotary(value_matrix, cosine_lookup, sine_lookup, head_count, sign_value):
    shaped = value_matrix.reshape(value_matrix.shape[0], head_count, HEAD_SIZE)
    lead_half = shaped[..., : HEAD_SIZE // 2]
    tail_half = shaped[..., HEAD_SIZE // 2 :]
    out_lead = lead_half * cosine_lookup - sign_value * tail_half * sine_lookup
    out_tail = tail_half * cosine_lookup + sign_value * lead_half * sine_lookup
    return jnp.concatenate([out_lead, out_tail], axis=-1).reshape(
        value_matrix.shape[0], head_count * HEAD_SIZE
    )


def divide_pair(value_matrix):
    high = value_matrix.astype(jnp.bfloat16)
    high = lax.optimization_barrier(high)
    low = (value_matrix - high.astype(jnp.float32)).astype(jnp.bfloat16)
    return high.astype(jnp.float32) + low.astype(jnp.float32)


VMEM_LIMIT = 56 * 1024 * 1024


class Place:
    def __init__(self, span):
        self.tok = lax.axis_index("tok")
        self.feat = lax.axis_index("feat")
        self.span = span
        tok_count, feat_count = lax.axis_size("tok"), lax.axis_size("feat")
        self.sizes = {"k": tok_count // 2, "ks": span // 2, "y": 2, "x": feat_count // 2, "c": 2}
        within = lax.rem(self.tok, span)
        self.base = self.tok - within
        self.at = {
            "k": lax.div(self.tok, 2),
            "ks": lax.div(within, 2),
            "y": lax.rem(self.tok, 2),
            "x": lax.div(self.feat, 2),
            "c": lax.rem(self.feat, 2),
        }

    def moved(self, dim, step):
        return lax.rem(self.at[dim] + step, self.sizes[dim])

    def index(self, offsets):
        result = 0
        for dim in ("k", "ks", "y", "x", "c"):
            if dim in offsets:
                result = result * self.sizes[dim] + self.moved(dim, offsets[dim])
        return result

    def peer(self, dim, step):
        tok, feat = self.tok, self.feat
        value = self.moved(dim, step)
        if dim == "k":
            tok = value * 2 + self.at["y"]
        elif dim == "ks":
            tok = self.base + value * 2 + self.at["y"]
        elif dim == "y":
            tok = self.at["k"] * 2 + value
        elif dim == "x":
            feat = value * 2 + self.at["c"]
        else:
            feat = self.at["x"] * 2 + value
        return {"tok": tok, "feat": feat}


def greet(place, dims):
    barrier = pltpu.get_barrier_semaphore()
    count = 0
    for dim in dims:
        for step in range(1, place.sizes[dim]):
            pl.semaphore_signal(
                barrier,
                inc=1,
                device_id=place.peer(dim, step),
                device_id_type=pl.DeviceIdType.MESH,
            )
            count += 1
    pl.semaphore_wait(barrier, count)


def all_dims(jobs):
    return [dim for dim in ("k", "ks", "y", "x", "c") if any(dim in job for job in jobs)]


def dim_sizes(span):
    return {
        "k": lax.axis_size("tok") // 2,
        "ks": span // 2,
        "y": 2,
        "x": lax.axis_size("feat") // 2,
        "c": 2,
    }


def staged_gather(arrays, jobs, collective, span):
    sizes = dim_sizes(span)
    count = len(arrays)
    slots = {}
    for j, dims in enumerate(jobs):
        for s, dim in enumerate(dims):
            for held in itertools.product(*[range(sizes[d]) for d in dims[:s]]):
                for step in range(1, sizes[dim]):
                    slots[j, s, held, step] = len(slots)
    totals = [math.prod(sizes[d] for d in dims) for dims in jobs]

    def kernel(*refs):
        ins, outs = refs[:count], refs[count : 2 * count]
        send_sem, recv_sem, local_sem = refs[2 * count :]
        place = Place(span)
        greet(place, all_dims(jobs))

        def block(j, held):
            dims = jobs[j]
            offsets = dict(zip(dims, tuple(held) + (0,) * (len(dims) - len(held))))
            return outs[j].at[place.index(offsets)]

        def copy(j, s, held, step, src, dst):
            slot = slots[j, s, held, step]
            return pltpu.make_async_remote_copy(
                src_ref=src,
                dst_ref=dst,
                send_sem=send_sem.at[slot],
                recv_sem=recv_sem.at[slot],
                device_id=place.peer(jobs[j][s], step),
                device_id_type=pl.DeviceIdType.MESH,
            )

        sent = []

        def forward(j, held, first, src):
            dims = jobs[j]
            for s in range(first, len(dims)):
                padded = held + (0,) * (s - len(held))
                for step in range(1, sizes[dims[s]]):
                    moving = copy(j, s, padded, step, src, block(j, padded))
                    moving.start()
                    sent.append(moving)

        local = []
        for j in range(count):
            forward(j, (), 0, ins[j])
            own = pltpu.make_async_copy(ins[j], block(j, ()), local_sem.at[j])
            own.start()
            local.append(own)
        for s in range(max(len(dims) for dims in jobs)):
            for j, dims in enumerate(jobs):
                if s >= len(dims):
                    continue
                size = sizes[dims[s]]
                for held in itertools.product(*[range(sizes[d]) for d in dims[:s]]):
                    for step in range(1, size):
                        arrived = held + ((size - step) % size,)
                        landed = block(j, arrived)
                        copy(j, s, held, step, landed, landed).wait_recv()
                        forward(j, arrived, s + 1, landed)
        for moving in sent:
            moving.wait_send()
        for own in local:
            own.wait()

    return pl.pallas_call(
        kernel,
        out_shape=[
            jax.ShapeDtypeStruct((total,) + a.shape, a.dtype) for total, a in zip(totals, arrays)
        ],
        in_specs=[pl.BlockSpec(memory_space=pl.ANY)] * count,
        out_specs=[pl.BlockSpec(memory_space=pl.ANY)] * count,
        scratch_shapes=[
            pltpu.SemaphoreType.DMA((len(slots),)),
            pltpu.SemaphoreType.DMA((len(slots),)),
            pltpu.SemaphoreType.DMA((count,)),
        ],
        compiler_params=pltpu.CompilerParams(collective_id=collective, has_side_effects=True),
    )(*arrays)


def staged_reduce(arrays, jobs, collective, span):
    sizes = dim_sizes(span)
    count = len(arrays)
    slots, scratch, where = {}, [], {}
    for j, dims in enumerate(jobs):
        tile = arrays[j].shape[1:]
        for s in range(len(dims)):
            rest = math.prod(sizes[d] for d in dims[s + 1 :])
            for step in range(1, sizes[dims[s]]):
                for held in itertools.product(*[range(sizes[d]) for d in dims[s + 1 :]]):
                    slots[j, s, step, held] = len(slots)
            where["recv", j, s] = len(scratch)
            scratch.append(pltpu.VMEM(((sizes[dims[s]] - 1) * rest,) + tile, jnp.bfloat16))
            if s < len(dims) - 1:
                where["sum", j, s] = len(scratch)
                scratch.append(pltpu.VMEM((rest,) + tile, jnp.bfloat16))

    def flat(dims, held):
        result = 0
        for d, offset in zip(dims, held):
            result = result * sizes[d] + offset
        return result

    def kernel(*refs):
        ins, outs = refs[:count], refs[count : 2 * count]
        buffers = refs[2 * count : 2 * count + len(scratch)]
        send_sem, recv_sem = refs[2 * count + len(scratch) :]
        place = Place(span)
        greet(place, all_dims(jobs))

        def source(j, s, held):
            dims = jobs[j]
            if s == 0:
                return ins[j].at[place.index(dict(zip(dims, held)))]
            return buffers[where["sum", j, s - 1]].at[flat(dims[s:], held)]

        def landing(j, s, step, held):
            dims = jobs[j]
            rest = math.prod(sizes[d] for d in dims[s + 1 :])
            return buffers[where["recv", j, s]].at[(step - 1) * rest + flat(dims[s + 1 :], held)]

        def copy(j, s, step, held):
            slot = slots[j, s, step, held]
            return pltpu.make_async_remote_copy(
                src_ref=source(j, s, (step,) + held),
                dst_ref=landing(j, s, step, held),
                send_sem=send_sem.at[slot],
                recv_sem=recv_sem.at[slot],
                device_id=place.peer(jobs[j][s], step),
                device_id_type=pl.DeviceIdType.MESH,
            )

        sent = []

        def start(j, s, step, held):
            moving = copy(j, s, step, held)
            moving.start()
            sent.append(moving)

        def offsets_of(dims):
            return reversed(list(itertools.product(*[range(sizes[d]) for d in dims])))

        for j, dims in enumerate(jobs):
            for held in offsets_of(dims[1:]):
                for step in range(1, sizes[dims[0]]):
                    start(j, 0, step, held)
        for s in range(max(len(dims) for dims in jobs)):
            for j, dims in enumerate(jobs):
                if s >= len(dims):
                    continue
                last = s == len(dims) - 1
                for held in offsets_of(dims[s + 1 :]):
                    steps = range(1, sizes[dims[s]])
                    for step in steps:
                        copy(j, s, step, held).wait_recv()
                    own = source(j, s, (0,) + held)
                    parts = [landing(j, s, step, held) for step in steps]
                    into = outs[j] if last else buffers[where["sum", j, s]].at[flat(dims[s + 1 :], held)]

                    @pl.loop(0, arrays[j].shape[1] // 16)
                    def _(chunk):
                        rows = pl.ds(pl.multiple_of(chunk * 16, 16), 16)
                        total = own[rows, :].astype(jnp.float32)
                        for part in parts:
                            total = total + part[rows, :].astype(jnp.float32)
                        into[rows, :] = total.astype(into.dtype)

                    if not last and held[0] != 0:
                        start(j, s + 1, held[0], held[1:])
        for moving in sent:
            moving.wait_send()

    return pl.pallas_call(
        kernel,
        out_shape=[jax.ShapeDtypeStruct(a.shape[1:], jnp.float32) for a in arrays],
        in_specs=[pl.BlockSpec(memory_space=pltpu.VMEM)] * count,
        out_specs=[pl.BlockSpec(memory_space=pltpu.VMEM)] * count,
        scratch_shapes=scratch
        + [pltpu.SemaphoreType.DMA((len(slots),)), pltpu.SemaphoreType.DMA((len(slots),))],
        compiler_params=pltpu.CompilerParams(
            collective_id=collective, has_side_effects=True, vmem_limit_bytes=VMEM_LIMIT
        ),
    )(*arrays)


def on_device(
    inputs, attn_gain, w_query, w_key, value_weight, w_out, ffn_gain, w_gate, w_up, w_down, cot
):
    f32, bf16 = jnp.float32, jnp.bfloat16
    token_rows, own_width = inputs.shape
    feat_count = lax.axis_size("feat")
    tok_count = lax.axis_size("tok")
    local_rows = token_rows // feat_count
    span = SEQ_LEN // token_rows
    query_width = QUERY_HEADS * HEAD_SIZE
    kv_width = KEY_HEADS * HEAD_SIZE
    qkv_width = query_width + 2 * kv_width
    score_scale = 1.0 / math.sqrt(HEAD_SIZE)
    feat_index = lax.axis_index("feat")
    depth = lax.rem(lax.axis_index("tok"), span)
    own_first = feat_index * local_rows
    rows = depth * token_rows + own_first + jnp.arange(local_rows, dtype=jnp.int32)
    cosine_lookup, sine_lookup = rotary_tables(rows)
    ff_own = w_gate.shape[1]
    out_rows = w_out.shape[0]
    padded_rows = -(-(out_rows + 1) // 16) * 16

    def padded(a):
        return jnp.pad(a, ((0, padded_rows - out_rows), (0, 0)))

    tok_dims, feat_dims = ("k", "y"), ("x", "c")
    qkv_shards, inputs_g, wo_shards, cot_g, gains_g, gate_up_shards, down_shards = staged_gather(
        [
            jnp.concatenate([w_query, w_key, value_weight], axis=1),
            inputs,
            padded(w_out),
            cot,
            jnp.broadcast_to(ffn_gain[None], (8, own_width)),
            padded(jnp.concatenate([w_gate, w_up], axis=1)),
            w_down,
        ],
        [tok_dims, feat_dims, tok_dims + feat_dims, feat_dims, feat_dims, tok_dims, tok_dims],
        0,
        span,
    )
    q_part, k_part = w_query.shape[1], w_key.shape[1]
    shard_columns = qkv_shards.transpose(1, 0, 2)
    qkv_weights = jnp.concatenate(
        [
            shard_columns[:, :, :q_part].reshape(own_width, query_width),
            shard_columns[:, :, q_part : q_part + k_part].reshape(own_width, kv_width),
            shard_columns[:, :, q_part + k_part :].reshape(own_width, kv_width),
        ],
        axis=1,
    )
    inputs_all = inputs_g.transpose(1, 0, 2).reshape(token_rows, MODEL_WIDTH)
    cot_all = cot_g.transpose(1, 0, 2).reshape(token_rows, MODEL_WIDTH)
    gain_all = gains_g[:, 0].reshape(MODEL_WIDTH)
    wo_all = (
        wo_shards.reshape(tok_count, feat_count, padded_rows, own_width)[:, :, :out_rows]
        .transpose(0, 2, 1, 3)
        .reshape(query_width, MODEL_WIDTH)
    )
    gate_up = gate_up_shards[:, :out_rows].reshape(MODEL_WIDTH, 2 * ff_own)
    wd_loc = down_shards.transpose(1, 0, 2).reshape(ff_own, MODEL_WIDTH)

    inputs_all_wide = inputs_all.astype(f32)
    inputs_wide = inputs.astype(f32)
    scale_one = lax.rsqrt(jnp.mean(inputs_all_wide * inputs_all_wide, axis=1, keepdims=True) + EPS)
    normed_one = (inputs_wide * scale_one * attn_gain[None, :]).astype(bf16)
    (projection,) = staged_reduce(
        [
            jnp.dot(normed_one, qkv_weights, preferred_element_type=f32)
            .astype(bf16)
            .reshape(feat_count, local_rows, qkv_width)
        ],
        [("c", "x")],
        1,
        span,
    )
    queries = apply_rotary(
        projection[:, :query_width], cosine_lookup, sine_lookup, QUERY_HEADS, 1.0
    ).astype(bf16)
    keys = apply_rotary(
        projection[:, query_width : query_width + kv_width],
        cosine_lookup,
        sine_lookup,
        KEY_HEADS,
        1.0,
    ).astype(bf16)
    values = projection[:, query_width + kv_width :].astype(bf16)
    (kv_shards,) = staged_gather(
        [jnp.concatenate([keys, values], axis=1)], [("ks", "y", "x", "c")], 2, span
    )
    kv_blocks = kv_shards.reshape(span, token_rows, 2 * kv_width)
    query_rows = queries.reshape(local_rows, KEY_HEADS, QUERY_PER_KEY, HEAD_SIZE).transpose(
        1, 2, 0, 3
    )

    def block_of(turn):
        piece = lax.dynamic_index_in_dim(kv_blocks, turn, 0, keepdims=False)
        return (
            piece[:, :kv_width].reshape(token_rows, KEY_HEADS, HEAD_SIZE),
            piece[:, kv_width:].reshape(token_rows, KEY_HEADS, HEAD_SIZE),
        )

    def allowed_of(turn):
        key_pos = turn * token_rows + jnp.arange(token_rows, dtype=jnp.int32)
        return key_pos[None, :] <= rows[:, None]

    def attend(turn, carried):
        maxima, totals, weighted = carried
        key_set, value_set = block_of(turn)
        scores = (
            jnp.einsum("gcrd,ngd->gcrn", query_rows, key_set, preferred_element_type=f32)
            * score_scale
        )
        masked = jnp.where(allowed_of(turn), scores, LARGE_NEGATIVE)
        new_max = jnp.maximum(maxima, jnp.max(masked, axis=-1))
        weights = jnp.exp(masked - new_max[..., None])
        factor = jnp.exp(maxima - new_max)
        return (
            new_max,
            totals * factor + jnp.sum(weights, axis=-1),
            weighted * factor[..., None]
            + jnp.einsum(
                "gcrn,ngd->gcrd", weights.astype(bf16), value_set, preferred_element_type=f32
            ),
        )

    state = (KEY_HEADS, QUERY_PER_KEY, local_rows)
    maxima, totals, weighted = lax.fori_loop(
        0,
        depth + 1,
        attend,
        (
            jnp.full(state, LARGE_NEGATIVE, f32),
            jnp.zeros(state, f32),
            jnp.zeros(state + (HEAD_SIZE,), f32),
        ),
    )
    heads_rows = (weighted / totals[..., None]).astype(bf16)
    heads_out = heads_rows.transpose(2, 0, 1, 3).reshape(local_rows, query_width)
    log_used = divide_pair(maxima + jnp.log(totals))
    (heads_g,) = staged_gather([heads_out], [feat_dims], 3, span)
    heads_all = heads_g.reshape(token_rows, query_width)

    residual_all = inputs_all_wide + jnp.dot(heads_all, wo_all, preferred_element_type=f32)
    scale_two = lax.rsqrt(jnp.mean(residual_all * residual_all, axis=1, keepdims=True) + EPS)
    normed_two = (residual_all * scale_two * gain_all[None, :]).astype(bf16)
    gate_up_pre = jnp.dot(normed_two, gate_up, preferred_element_type=f32)
    gate_pre, up_pre = gate_up_pre[:, :ff_own], gate_up_pre[:, ff_own:]
    sigmoid_gate = jax.nn.sigmoid(gate_pre)
    hidden = (gate_pre * sigmoid_gate * up_pre).astype(bf16)
    ffn_partial = jnp.dot(hidden, wd_loc, preferred_element_type=f32).astype(bf16)
    grad_down = jnp.dot(hidden.T, cot_all, preferred_element_type=f32)
    d_hidden = jnp.dot(cot_all, wd_loc.T, preferred_element_type=f32)
    d_gate = (d_hidden * up_pre * sigmoid_gate * (1.0 + gate_pre * (1.0 - sigmoid_gate))).astype(
        bf16
    )
    d_up = (d_hidden * gate_pre * sigmoid_gate).astype(bf16)
    d_gate_up = jnp.concatenate([d_gate, d_up], axis=1)
    grad_gate_up = jnp.dot(normed_two.T, d_gate_up, preferred_element_type=f32)
    back_two = jnp.dot(d_gate_up, gate_up.T, preferred_element_type=f32).astype(bf16)
    d_norm_two, ffn_term = staged_reduce(
        [
            back_two.reshape(feat_count, local_rows, MODEL_WIDTH),
            ffn_partial.reshape(token_rows, feat_count, own_width).transpose(1, 0, 2),
        ],
        [("c", "x"), ("c", "x")],
        4,
        span,
    )
    residual_own = lax.dynamic_slice_in_dim(
        residual_all, feat_index * own_width, own_width, 1
    )
    block_out = residual_own + ffn_term

    def own_rows(a):
        return lax.dynamic_slice_in_dim(a, own_first, local_rows, 0)

    residual_rows, scale_rows = own_rows(residual_all), own_rows(scale_two)
    stat_two = jnp.sum(d_norm_two * gain_all[None, :] * residual_rows, axis=1, keepdims=True)
    d_mid_rows = (
        own_rows(cot_all).astype(f32)
        + scale_rows * gain_all[None, :] * d_norm_two
        - residual_rows * scale_rows**3 * stat_two / MODEL_WIDTH
    ).astype(bf16)
    gain_two_rows = jnp.sum(d_norm_two * residual_rows * scale_rows, axis=0)
    head_gradient = (
        jnp.dot(d_mid_rows, wo_all.T, preferred_element_type=f32)
        .astype(bf16)
        .reshape(local_rows, KEY_HEADS, QUERY_PER_KEY, HEAD_SIZE)
        .transpose(1, 2, 0, 3)
    )
    delta_used = divide_pair(
        jnp.sum(head_gradient.astype(f32) * heads_rows.astype(f32), axis=-1)
    )

    def backprop(turn, carried):
        query_sum, gradients = carried
        key_set, value_set = block_of(turn)
        scores = (
            jnp.einsum("gcrd,ngd->gcrn", query_rows, key_set, preferred_element_type=f32)
            * score_scale
        )
        masked = jnp.where(allowed_of(turn), scores, LARGE_NEGATIVE)
        probability = jnp.exp(masked - log_used[..., None])
        d_probs = jnp.einsum(
            "gcrd,ngd->gcrn", head_gradient, value_set, preferred_element_type=f32
        )
        d_scores = (probability * (d_probs - delta_used[..., None])).astype(bf16)
        query_sum = (
            query_sum
            + jnp.einsum("gcrn,ngd->gcrd", d_scores, key_set, preferred_element_type=f32)
            * score_scale
        )
        key_part = (
            jnp.einsum("gcrn,gcrd->ngd", d_scores, query_rows, preferred_element_type=f32)
            * score_scale
        )
        value_part = jnp.einsum(
            "gcrn,gcrd->ngd",
            probability.astype(bf16),
            head_gradient,
            preferred_element_type=f32,
        )
        part = jnp.concatenate(
            [key_part.reshape(token_rows, kv_width), value_part.reshape(token_rows, kv_width)],
            axis=1,
        ).astype(bf16)
        return (query_sum, lax.dynamic_update_index_in_dim(gradients, part, turn, 0))

    query_sum, gradients = lax.fori_loop(
        0,
        depth + 1,
        backprop,
        (
            jnp.zeros(state + (HEAD_SIZE,), f32),
            jnp.zeros((span, token_rows, 2 * kv_width), bf16),
        ),
    )
    (kv_gradient,) = staged_reduce(
        [gradients.reshape(span * feat_count, local_rows, 2 * kv_width)],
        [("c", "x", "y", "ks")],
        5,
        span,
    )
    d_qkv_rows = jnp.concatenate(
        [
            apply_rotary(
                query_sum.transpose(2, 0, 1, 3).reshape(local_rows, query_width),
                cosine_lookup,
                sine_lookup,
                QUERY_HEADS,
                -1.0,
            ),
            apply_rotary(
                kv_gradient[:, :kv_width], cosine_lookup, sine_lookup, KEY_HEADS, -1.0
            ),
            kv_gradient[:, kv_width:],
        ],
        axis=1,
    ).astype(bf16)
    d_qkv_g, d_mid_g, gain_two_g = staged_gather(
        [d_qkv_rows, d_mid_rows, jnp.broadcast_to(gain_two_rows[None], (8, MODEL_WIDTH))],
        [feat_dims, feat_dims, feat_dims],
        6,
        span,
    )
    d_qkv_all = d_qkv_g.reshape(token_rows, qkv_width)
    d_mid_all = d_mid_g.reshape(token_rows, MODEL_WIDTH)
    d_attn = lax.dynamic_slice_in_dim(d_mid_all, feat_index * own_width, own_width, 1)
    gain_two_term = lax.dynamic_slice_in_dim(
        jnp.sum(gain_two_g[:, 0], axis=0), feat_index * own_width, own_width, 0
    )
    grad_out = jnp.dot(heads_all.T, d_attn, preferred_element_type=f32)
    projection_gradient = jnp.dot(normed_one.T, d_qkv_all, preferred_element_type=f32)
    back_one = jnp.dot(d_qkv_all, qkv_weights.T, preferred_element_type=f32)
    stat_own = jnp.sum(back_one * attn_gain[None, :] * inputs_wide, axis=1)
    (stat_g,) = staged_gather(
        [jnp.broadcast_to(stat_own[None], (8, token_rows))], [feat_dims], 7, span
    )
    stat_one = jnp.sum(stat_g[:, 0], axis=0)[:, None]
    grad_inputs = (
        d_attn.astype(f32)
        + scale_one * attn_gain[None, :] * back_one
        - inputs_wide * scale_one**3 * stat_one / MODEL_WIDTH
    )
    gain_one_term = jnp.sum(back_one * inputs_wide * scale_one, axis=0)

    def split_columns(a):
        return a.reshape(a.shape[0], tok_count, -1)

    qkv_term = jnp.concatenate(
        [
            split_columns(projection_gradient[:, :query_width]),
            split_columns(projection_gradient[:, query_width : query_width + kv_width]),
            split_columns(projection_gradient[:, query_width + kv_width :]),
        ],
        axis=2,
    ).transpose(1, 0, 2)
    down_term = split_columns(grad_down).transpose(1, 0, 2)
    rows_term = jnp.concatenate([grad_out, grad_gate_up], axis=1)
    rows_width = rows_term.shape[1]
    gains_row = jnp.pad(
        jnp.concatenate([gain_one_term, gain_two_term]), (0, rows_width - 2 * own_width)
    )
    rows_term = jnp.concatenate(
        [
            rows_term.reshape(tok_count, out_rows, rows_width),
            jnp.broadcast_to(gains_row[None, None], (tok_count, 1, rows_width)),
            jnp.zeros((tok_count, padded_rows - out_rows - 1, rows_width), f32),
        ],
        axis=1,
    )
    rows_sum, down_sum, qkv_sum = staged_reduce(
        [rows_term.astype(bf16), down_term.astype(bf16), qkv_term.astype(bf16)],
        [("y", "k")] * 3,
        8,
        span,
    )
    return (
        block_out.T,
        grad_inputs.T,
        rows_sum[out_rows, :own_width],
        qkv_sum[:, :q_part],
        qkv_sum[:, q_part : q_part + k_part],
        qkv_sum[:, q_part + k_part :],
        rows_sum[:out_rows, :own_width],
        rows_sum[out_rows, own_width : 2 * own_width],
        rows_sum[:out_rows, own_width : own_width + ff_own],
        rows_sum[:out_rows, own_width + ff_own :],
        down_sum,
    )


def solution(mesh):
    return jax.shard_map(
        on_device,
        mesh=mesh,
        in_specs=(
            P("tok", "feat"),
            P("feat"),
            P("feat", "tok"),
            P("feat", "tok"),
            P("feat", "tok"),
            P("tok", "feat"),
            P("feat"),
            P("tok", "feat"),
            P("tok", "feat"),
            P("feat", "tok"),
            P("tok", "feat"),
        ),
        out_specs=(
            P("feat", "tok"),
            P("feat", "tok"),
            P("feat"),
            P("feat", "tok"),
            P("feat", "tok"),
            P("feat", "tok"),
            P("tok", "feat"),
            P("feat"),
            P("tok", "feat"),
            P("tok", "feat"),
            P("feat", "tok"),
        ),
        check_vma=False,
    )
```

```python
import itertools
import math

import jax
import jax.numpy as jnp
from jax import lax
from jax.experimental import pallas as pl
from jax.experimental.pallas import tpu as pltpu
from jax.sharding import PartitionSpec as P

MODEL_WIDTH = 960
QUERY_HEADS = 15
KEY_HEADS = 5
HEAD_SIZE = 64
SEQ_LEN = 4096
QUERY_PER_KEY = 3


EPS = 1e-05
ROPE_BASE = 10000.0
LARGE_NEGATIVE = -1e30


def rotary_tables(positions):
    half_width = HEAD_SIZE // 2
    inverse_freq = ROPE_BASE ** (-2.0 * jnp.arange(half_width, dtype=jnp.float32) / HEAD_SIZE)
    angles = positions.astype(jnp.float32)[:, None] * inverse_freq[None, :]
    return (jnp.cos(angles)[:, None, :], jnp.sin(angles)[:, None, :])


def apply_rotary(value_matrix, cosine_lookup, sine_lookup, head_count, sign_value):
    shaped = value_matrix.reshape(value_matrix.shape[0], head_count, HEAD_SIZE)
    lead_half = shaped[..., : HEAD_SIZE // 2]
    tail_half = shaped[..., HEAD_SIZE // 2 :]
    out_lead = lead_half * cosine_lookup - sign_value * tail_half * sine_lookup
    out_tail = tail_half * cosine_lookup + sign_value * lead_half * sine_lookup
    return jnp.concatenate([out_lead, out_tail], axis=-1).reshape(
        value_matrix.shape[0], head_count * HEAD_SIZE
    )


def divide_pair(value_matrix):
    high = value_matrix.astype(jnp.bfloat16)
    high = lax.optimization_barrier(high)
    low = (value_matrix - high.astype(jnp.float32)).astype(jnp.bfloat16)
    return high.astype(jnp.float32) + low.astype(jnp.float32)


VMEM_LIMIT = 56 * 1024 * 1024


class Place:
    def __init__(self, span):
        self.tok = lax.axis_index("tok")
        self.feat = lax.axis_index("feat")
        self.span = span
        tok_count, feat_count = lax.axis_size("tok"), lax.axis_size("feat")
        self.sizes = {"k": tok_count // 2, "ks": span // 2, "y": 2, "x": feat_count // 2, "c": 2}
        within = lax.rem(self.tok, span)
        self.base = self.tok - within
        self.at = {
            "k": lax.div(self.tok, 2),
            "ks": lax.div(within, 2),
            "y": lax.rem(self.tok, 2),
            "x": lax.div(self.feat, 2),
            "c": lax.rem(self.feat, 2),
        }

    def moved(self, dim, step):
        return lax.rem(self.at[dim] + step, self.sizes[dim])

    def index(self, offsets):
        result = 0
        for dim in ("k", "ks", "y", "x", "c"):
            if dim in offsets:
                result = result * self.sizes[dim] + self.moved(dim, offsets[dim])
        return result

    def peer(self, dim, step):
        tok, feat = self.tok, self.feat
        value = self.moved(dim, step)
        if dim == "k":
            tok = value * 2 + self.at["y"]
        elif dim == "ks":
            tok = self.base + value * 2 + self.at["y"]
        elif dim == "y":
            tok = self.at["k"] * 2 + value
        elif dim == "x":
            feat = value * 2 + self.at["c"]
        else:
            feat = self.at["x"] * 2 + value
        return {"tok": tok, "feat": feat}


def greet(place, dims):
    barrier = pltpu.get_barrier_semaphore()
    count = 0
    for dim in dims:
        for step in range(1, place.sizes[dim]):
            pl.semaphore_signal(
                barrier,
                inc=1,
                device_id=place.peer(dim, step),
                device_id_type=pl.DeviceIdType.MESH,
            )
            count += 1
    pl.semaphore_wait(barrier, count)


def all_dims(jobs):
    return [dim for dim in ("k", "ks", "y", "x", "c") if any(dim in job for job in jobs)]


def dim_sizes(span):
    return {
        "k": lax.axis_size("tok") // 2,
        "ks": span // 2,
        "y": 2,
        "x": lax.axis_size("feat") // 2,
        "c": 2,
    }


def staged_gather(arrays, jobs, collective, span):
    sizes = dim_sizes(span)
    count = len(arrays)
    slots = {}
    for j, dims in enumerate(jobs):
        for s, dim in enumerate(dims):
            for held in itertools.product(*[range(sizes[d]) for d in dims[:s]]):
                for step in range(1, sizes[dim]):
                    slots[j, s, held, step] = len(slots)
    totals = [math.prod(sizes[d] for d in dims) for dims in jobs]

    def kernel(*refs):
        ins, outs = refs[:count], refs[count : 2 * count]
        send_sem, recv_sem, local_sem = refs[2 * count :]
        place = Place(span)
        greet(place, all_dims(jobs))

        def block(j, held):
            dims = jobs[j]
            offsets = dict(zip(dims, tuple(held) + (0,) * (len(dims) - len(held))))
            return outs[j].at[place.index(offsets)]

        def copy(j, s, held, step, src, dst):
            slot = slots[j, s, held, step]
            return pltpu.make_async_remote_copy(
                src_ref=src,
                dst_ref=dst,
                send_sem=send_sem.at[slot],
                recv_sem=recv_sem.at[slot],
                device_id=place.peer(jobs[j][s], step),
                device_id_type=pl.DeviceIdType.MESH,
            )

        sent = []

        def forward(j, held, first, src):
            dims = jobs[j]
            for s in range(first, len(dims)):
                padded = held + (0,) * (s - len(held))
                for step in range(1, sizes[dims[s]]):
                    moving = copy(j, s, padded, step, src, block(j, padded))
                    moving.start()
                    sent.append(moving)

        local = []
        for j in range(count):
            forward(j, (), 0, ins[j])
            own = pltpu.make_async_copy(ins[j], block(j, ()), local_sem.at[j])
            own.start()
            local.append(own)
        for s in range(max(len(dims) for dims in jobs)):
            for j, dims in enumerate(jobs):
                if s >= len(dims):
                    continue
                size = sizes[dims[s]]
                for held in itertools.product(*[range(sizes[d]) for d in dims[:s]]):
                    for step in range(1, size):
                        arrived = held + ((size - step) % size,)
                        landed = block(j, arrived)
                        copy(j, s, held, step, landed, landed).wait_recv()
                        forward(j, arrived, s + 1, landed)
        for moving in sent:
            moving.wait_send()
        for own in local:
            own.wait()

    return pl.pallas_call(
        kernel,
        out_shape=[
            jax.ShapeDtypeStruct((total,) + a.shape, a.dtype) for total, a in zip(totals, arrays)
        ],
        in_specs=[pl.BlockSpec(memory_space=pl.ANY)] * count,
        out_specs=[pl.BlockSpec(memory_space=pl.ANY)] * count,
        scratch_shapes=[
            pltpu.SemaphoreType.DMA((len(slots),)),
            pltpu.SemaphoreType.DMA((len(slots),)),
            pltpu.SemaphoreType.DMA((count,)),
        ],
        compiler_params=pltpu.CompilerParams(collective_id=collective, has_side_effects=True),
    )(*arrays)


def staged_reduce(arrays, jobs, collective, span):
    sizes = dim_sizes(span)
    count = len(arrays)
    slots, scratch, where = {}, [], {}
    for j, dims in enumerate(jobs):
        tile = arrays[j].shape[1:]
        for s in range(len(dims)):
            rest = math.prod(sizes[d] for d in dims[s + 1 :])
            for step in range(1, sizes[dims[s]]):
                for held in itertools.product(*[range(sizes[d]) for d in dims[s + 1 :]]):
                    slots[j, s, step, held] = len(slots)
            where["recv", j, s] = len(scratch)
            scratch.append(pltpu.VMEM(((sizes[dims[s]] - 1) * rest,) + tile, jnp.bfloat16))
            if s < len(dims) - 1:
                where["sum", j, s] = len(scratch)
                scratch.append(pltpu.VMEM((rest,) + tile, jnp.bfloat16))

    def flat(dims, held):
        result = 0
        for d, offset in zip(dims, held):
            result = result * sizes[d] + offset
        return result

    def kernel(*refs):
        ins, outs = refs[:count], refs[count : 2 * count]
        buffers = refs[2 * count : 2 * count + len(scratch)]
        send_sem, recv_sem = refs[2 * count + len(scratch) :]
        place = Place(span)
        greet(place, all_dims(jobs))

        def source(j, s, held):
            dims = jobs[j]
            if s == 0:
                return ins[j].at[place.index(dict(zip(dims, held)))]
            return buffers[where["sum", j, s - 1]].at[flat(dims[s:], held)]

        def landing(j, s, step, held):
            dims = jobs[j]
            rest = math.prod(sizes[d] for d in dims[s + 1 :])
            return buffers[where["recv", j, s]].at[(step - 1) * rest + flat(dims[s + 1 :], held)]

        def copy(j, s, step, held):
            slot = slots[j, s, step, held]
            return pltpu.make_async_remote_copy(
                src_ref=source(j, s, (step,) + held),
                dst_ref=landing(j, s, step, held),
                send_sem=send_sem.at[slot],
                recv_sem=recv_sem.at[slot],
                device_id=place.peer(jobs[j][s], step),
                device_id_type=pl.DeviceIdType.MESH,
            )

        sent = []

        def start(j, s, step, held):
            moving = copy(j, s, step, held)
            moving.start()
            sent.append(moving)

        def offsets_of(dims):
            return reversed(list(itertools.product(*[range(sizes[d]) for d in dims])))

        for j, dims in enumerate(jobs):
            for held in offsets_of(dims[1:]):
                for step in range(1, sizes[dims[0]]):
                    start(j, 0, step, held)
        for s in range(max(len(dims) for dims in jobs)):
            for j, dims in enumerate(jobs):
                if s >= len(dims):
                    continue
                last = s == len(dims) - 1
                for held in offsets_of(dims[s + 1 :]):
                    steps = range(1, sizes[dims[s]])
                    for step in steps:
                        copy(j, s, step, held).wait_recv()
                    own = source(j, s, (0,) + held)
                    parts = [landing(j, s, step, held) for step in steps]
                    into = outs[j] if last else buffers[where["sum", j, s]].at[flat(dims[s + 1 :], held)]

                    @pl.loop(0, arrays[j].shape[1] // 16)
                    def _(chunk):
                        rows = pl.ds(pl.multiple_of(chunk * 16, 16), 16)
                        total = own[rows, :].astype(jnp.float32)
                        for part in parts:
                            total = total + part[rows, :].astype(jnp.float32)
                        into[rows, :] = total.astype(into.dtype)

                    if not last and held[0] != 0:
                        start(j, s + 1, held[0], held[1:])
        for moving in sent:
            moving.wait_send()

    return pl.pallas_call(
        kernel,
        out_shape=[jax.ShapeDtypeStruct(a.shape[1:], jnp.float32) for a in arrays],
        in_specs=[pl.BlockSpec(memory_space=pltpu.VMEM)] * count,
        out_specs=[pl.BlockSpec(memory_space=pltpu.VMEM)] * count,
        scratch_shapes=scratch
        + [pltpu.SemaphoreType.DMA((len(slots),)), pltpu.SemaphoreType.DMA((len(slots),))],
        compiler_params=pltpu.CompilerParams(
            collective_id=collective, has_side_effects=True, vmem_limit_bytes=VMEM_LIMIT
        ),
    )(*arrays)


def moved_along(value, axis, step):
    count = lax.axis_size(axis)
    return lax.ppermute(value, axis, [(i, (i + step) % count) for i in range(count)])


def placed_along(parts, axis):
    count = lax.axis_size(axis)
    index = lax.axis_index(axis)
    result = jnp.zeros((count,) + parts[0].shape, parts[0].dtype)
    for step, part in enumerate(parts):
        result = lax.dynamic_update_index_in_dim(
            result, part, lax.rem(index + count - step, count), 0
        )
    return result


def exchanged_along(blocks, axis):
    count = lax.axis_size(axis)
    index = lax.axis_index(axis)

    def picked(step):
        return lax.dynamic_index_in_dim(blocks, lax.rem(index + step, count), 0, keepdims=False)

    return [picked(0)] + [moved_along(picked(step), axis, step) for step in range(1, count)]


def on_device(
    inputs, attn_gain, w_query, w_key, value_weight, w_out, ffn_gain, w_gate, w_up, w_down, cot
):
    f32, bf16 = jnp.float32, jnp.bfloat16
    token_rows, own_width = inputs.shape
    feat_count = lax.axis_size("feat")
    tok_count = lax.axis_size("tok")
    local_rows = token_rows // feat_count
    span = SEQ_LEN // token_rows
    query_width = QUERY_HEADS * HEAD_SIZE
    kv_width = KEY_HEADS * HEAD_SIZE
    qkv_width = query_width + 2 * kv_width
    score_scale = 1.0 / math.sqrt(HEAD_SIZE)
    feat_index = lax.axis_index("feat")
    depth = lax.rem(lax.axis_index("tok"), span)
    own_first = feat_index * local_rows
    rows = depth * token_rows + own_first + jnp.arange(local_rows, dtype=jnp.int32)
    cosine_lookup, sine_lookup = rotary_tables(rows)
    ff_own = w_gate.shape[1]
    out_rows = w_out.shape[0]
    padded_rows = -(-(out_rows + 2) // 16) * 16

    def padded(a):
        return jnp.pad(a, ((0, padded_rows - out_rows), (0, 0)))

    tok_dims, feat_dims = ("k", "y"), ("x", "c")
    ffn_shard = jnp.concatenate([w_gate, w_up, w_down.T], axis=1)
    ffn_shards = [ffn_shard] + [
        moved_along(ffn_shard, "tok", step) for step in range(1, tok_count)
    ]
    early = -(-5 * tok_count // 8) + 1
    qkv_shards, inputs_g, wo_shards, cot_g, gains_g = staged_gather(
        [
            jnp.concatenate([w_query, w_key, value_weight], axis=1),
            inputs,
            padded(w_out),
            cot,
            jnp.broadcast_to(ffn_gain[None], (8, own_width)),
        ],
        [tok_dims, feat_dims, tok_dims + feat_dims, feat_dims, feat_dims],
        0,
        span,
    )
    q_part, k_part = w_query.shape[1], w_key.shape[1]
    shard_columns = qkv_shards.transpose(1, 0, 2)
    qkv_weights = jnp.concatenate(
        [
            shard_columns[:, :, :q_part].reshape(own_width, query_width),
            shard_columns[:, :, q_part : q_part + k_part].reshape(own_width, kv_width),
            shard_columns[:, :, q_part + k_part :].reshape(own_width, kv_width),
        ],
        axis=1,
    )
    inputs_all = inputs_g.transpose(1, 0, 2).reshape(token_rows, MODEL_WIDTH)
    cot_all = cot_g.transpose(1, 0, 2).reshape(token_rows, MODEL_WIDTH)
    gain_all = gains_g[:, 0].reshape(MODEL_WIDTH)
    wo_all = (
        wo_shards.reshape(tok_count, feat_count, padded_rows, own_width)[:, :, :out_rows]
        .transpose(0, 2, 1, 3)
        .reshape(query_width, MODEL_WIDTH)
    )

    inputs_all_wide = inputs_all.astype(f32)
    inputs_wide = inputs.astype(f32)
    scale_one = lax.rsqrt(jnp.mean(inputs_all_wide * inputs_all_wide, axis=1, keepdims=True) + EPS)
    normed_one = (inputs_wide * scale_one * attn_gain[None, :]).astype(bf16)
    (projection,) = staged_reduce(
        [
            jnp.dot(normed_one, qkv_weights, preferred_element_type=f32)
            .astype(bf16)
            .reshape(feat_count, local_rows, qkv_width)
        ],
        [("c", "x")],
        1,
        span,
    )
    queries = apply_rotary(
        projection[:, :query_width], cosine_lookup, sine_lookup, QUERY_HEADS, 1.0
    ).astype(bf16)
    keys = apply_rotary(
        projection[:, query_width : query_width + kv_width],
        cosine_lookup,
        sine_lookup,
        KEY_HEADS,
        1.0,
    ).astype(bf16)
    values = projection[:, query_width + kv_width :].astype(bf16)
    kv_own = jnp.concatenate([keys, values], axis=1)
    cut = min(-(-kv_width // 128) * 128, 2 * kv_width)
    kv_first, kv_second = staged_gather(
        [kv_own[:, :cut], kv_own[:, cut:]],
        [("ks", "y", "x", "c"), ("ks", "x", "y", "c")],
        2,
        span,
    )
    kv_blocks = jnp.concatenate([kv_first, kv_second], axis=2).reshape(
        span, token_rows, 2 * kv_width
    )
    kv_blocks, ffn_shards[:early] = lax.optimization_barrier((kv_blocks, ffn_shards[:early]))
    query_rows = queries.reshape(local_rows, KEY_HEADS, QUERY_PER_KEY, HEAD_SIZE).transpose(
        1, 2, 0, 3
    )

    def block_of(turn):
        piece = lax.dynamic_index_in_dim(kv_blocks, turn, 0, keepdims=False)
        return (
            piece[:, :kv_width].reshape(token_rows, KEY_HEADS, HEAD_SIZE),
            piece[:, kv_width:].reshape(token_rows, KEY_HEADS, HEAD_SIZE),
        )

    def allowed_of(turn):
        key_pos = turn * token_rows + jnp.arange(token_rows, dtype=jnp.int32)
        return key_pos[None, :] <= rows[:, None]

    def attend(turn, carried):
        maxima, totals, weighted = carried
        key_set, value_set = block_of(turn)
        scores = (
            jnp.einsum("gcrd,ngd->gcrn", query_rows, key_set, preferred_element_type=f32)
            * score_scale
        )
        masked = jnp.where(allowed_of(turn), scores, LARGE_NEGATIVE)
        new_max = jnp.maximum(maxima, jnp.max(masked, axis=-1))
        weights = jnp.exp(masked - new_max[..., None])
        factor = jnp.exp(maxima - new_max)
        return (
            new_max,
            totals * factor + jnp.sum(weights, axis=-1),
            weighted * factor[..., None]
            + jnp.einsum(
                "gcrn,ngd->gcrd", weights.astype(bf16), value_set, preferred_element_type=f32
            ),
        )

    state = (KEY_HEADS, QUERY_PER_KEY, local_rows)
    maxima, totals, weighted = lax.fori_loop(
        0,
        depth + 1,
        attend,
        (
            jnp.full(state, LARGE_NEGATIVE, f32),
            jnp.zeros(state, f32),
            jnp.zeros(state + (HEAD_SIZE,), f32),
        ),
    )
    heads_rows = (weighted / totals[..., None]).astype(bf16)
    heads_out = heads_rows.transpose(2, 0, 1, 3).reshape(local_rows, query_width)
    log_used = divide_pair(maxima + jnp.log(totals))
    (heads_g,) = staged_gather([heads_out], [feat_dims], 3, span)
    heads_all = heads_g.reshape(token_rows, query_width)

    ffn_weights = placed_along(ffn_shards, "tok").reshape(MODEL_WIDTH, 3 * ff_own)
    gate_up, down_turned = ffn_weights[:, : 2 * ff_own], ffn_weights[:, 2 * ff_own :]
    residual_all = inputs_all_wide + jnp.dot(heads_all, wo_all, preferred_element_type=f32)
    scale_two = lax.rsqrt(jnp.mean(residual_all * residual_all, axis=1, keepdims=True) + EPS)
    normed_two = (residual_all * scale_two * gain_all[None, :]).astype(bf16)
    gate_up_pre = jnp.dot(normed_two, gate_up, preferred_element_type=f32)
    gate_pre, up_pre = gate_up_pre[:, :ff_own], gate_up_pre[:, ff_own:]
    sigmoid_gate = jax.nn.sigmoid(gate_pre)
    hidden = (gate_pre * sigmoid_gate * up_pre).astype(bf16)
    ffn_partial = jnp.dot(hidden, down_turned.T, preferred_element_type=f32).astype(bf16)
    d_hidden = jnp.dot(cot_all, down_turned, preferred_element_type=f32)
    d_gate = (d_hidden * up_pre * sigmoid_gate * (1.0 + gate_pre * (1.0 - sigmoid_gate))).astype(
        bf16
    )
    d_up = (d_hidden * gate_pre * sigmoid_gate).astype(bf16)
    d_gate_up = jnp.concatenate([d_gate, d_up], axis=1)
    ffn_gradient = jnp.concatenate(
        [
            jnp.dot(normed_two.T, d_gate_up, preferred_element_type=f32).astype(bf16),
            jnp.dot(cot_all.T, hidden, preferred_element_type=f32).astype(bf16),
        ],
        axis=1,
    ).reshape(tok_count, out_rows, 3 * ff_own)
    ffn_parts = exchanged_along(ffn_gradient, "tok")
    back_two = jnp.dot(d_gate_up, gate_up.T, preferred_element_type=f32).astype(bf16)
    d_norm_two, ffn_term = staged_reduce(
        [
            back_two.reshape(feat_count, local_rows, MODEL_WIDTH),
            ffn_partial.reshape(token_rows, feat_count, own_width).transpose(1, 0, 2),
        ],
        [("c", "x"), ("c", "x")],
        4,
        span,
    )
    residual_own = lax.dynamic_slice_in_dim(
        residual_all, feat_index * own_width, own_width, 1
    )
    block_out = residual_own + ffn_term

    def own_rows(a):
        return lax.dynamic_slice_in_dim(a, own_first, local_rows, 0)

    residual_rows, scale_rows = own_rows(residual_all), own_rows(scale_two)
    stat_two = jnp.sum(d_norm_two * gain_all[None, :] * residual_rows, axis=1, keepdims=True)
    d_mid_rows = (
        own_rows(cot_all).astype(f32)
        + scale_rows * gain_all[None, :] * d_norm_two
        - residual_rows * scale_rows**3 * stat_two / MODEL_WIDTH
    ).astype(bf16)
    gain_two_rows = jnp.sum(d_norm_two * residual_rows * scale_rows, axis=0)
    head_gradient = (
        jnp.dot(d_mid_rows, wo_all.T, preferred_element_type=f32)
        .astype(bf16)
        .reshape(local_rows, KEY_HEADS, QUERY_PER_KEY, HEAD_SIZE)
        .transpose(1, 2, 0, 3)
    )
    delta_used = divide_pair(
        jnp.sum(head_gradient.astype(f32) * heads_rows.astype(f32), axis=-1)
    )

    def backprop(turn, carried):
        query_sum, gradients = carried
        key_set, value_set = block_of(turn)
        scores = (
            jnp.einsum("gcrd,ngd->gcrn", query_rows, key_set, preferred_element_type=f32)
            * score_scale
        )
        masked = jnp.where(allowed_of(turn), scores, LARGE_NEGATIVE)
        probability = jnp.exp(masked - log_used[..., None])
        d_probs = jnp.einsum(
            "gcrd,ngd->gcrn", head_gradient, value_set, preferred_element_type=f32
        )
        d_scores = (probability * (d_probs - delta_used[..., None])).astype(bf16)
        query_sum = (
            query_sum
            + jnp.einsum("gcrn,ngd->gcrd", d_scores, key_set, preferred_element_type=f32)
            * score_scale
        )
        key_part = (
            jnp.einsum("gcrn,gcrd->ngd", d_scores, query_rows, preferred_element_type=f32)
            * score_scale
        )
        value_part = jnp.einsum(
            "gcrn,gcrd->ngd",
            probability.astype(bf16),
            head_gradient,
            preferred_element_type=f32,
        )
        part = jnp.concatenate(
            [key_part.reshape(token_rows, kv_width), value_part.reshape(token_rows, kv_width)],
            axis=1,
        ).astype(bf16)
        return (query_sum, lax.dynamic_update_index_in_dim(gradients, part, turn, 0))

    query_sum, gradients = lax.fori_loop(
        0,
        depth + 1,
        backprop,
        (
            jnp.zeros(state + (HEAD_SIZE,), f32),
            jnp.zeros((span, token_rows, 2 * kv_width), bf16),
        ),
    )
    gradients, d_mid_rows, ffn_parts[:early] = lax.optimization_barrier(
        (gradients, d_mid_rows, ffn_parts[:early])
    )
    d_mid_parts = exchanged_along(
        d_mid_rows.reshape(local_rows, feat_count, own_width).transpose(1, 0, 2), "feat"
    )
    gradients = gradients.reshape(span * feat_count, local_rows, 2 * kv_width)
    kv_gradient = jnp.concatenate(
        staged_reduce(
            [gradients[:, :, :cut], gradients[:, :, cut:]],
            [("c", "x", "y", "ks"), ("c", "y", "x", "ks")],
            5,
            span,
        ),
        axis=1,
    )
    d_qkv_rows = jnp.concatenate(
        [
            apply_rotary(
                query_sum.transpose(2, 0, 1, 3).reshape(local_rows, query_width),
                cosine_lookup,
                sine_lookup,
                QUERY_HEADS,
                -1.0,
            ),
            apply_rotary(
                kv_gradient[:, :kv_width], cosine_lookup, sine_lookup, KEY_HEADS, -1.0
            ),
            kv_gradient[:, kv_width:],
        ],
        axis=1,
    ).astype(bf16)
    d_qkv_rows, d_mid_parts, ffn_parts[early:] = lax.optimization_barrier(
        (d_qkv_rows, d_mid_parts, ffn_parts[early:])
    )
    d_qkv_g, gain_two_g = staged_gather(
        [d_qkv_rows, jnp.broadcast_to(gain_two_rows[None], (8, MODEL_WIDTH))],
        [feat_dims, feat_dims],
        6,
        span,
    )
    d_qkv_all = d_qkv_g.reshape(token_rows, qkv_width)
    d_attn = placed_along(d_mid_parts, "feat")
    d_attn = d_attn.reshape(token_rows, own_width)
    gain_two_term = lax.dynamic_slice_in_dim(
        jnp.sum(gain_two_g[:, 0], axis=0), feat_index * own_width, own_width, 0
    )
    grad_out = jnp.dot(heads_all.T, d_attn, preferred_element_type=f32)
    projection_gradient = jnp.dot(normed_one.T, d_qkv_all, preferred_element_type=f32)
    back_one = jnp.dot(d_qkv_all, qkv_weights.T, preferred_element_type=f32)
    stat_own = jnp.sum(back_one * attn_gain[None, :] * inputs_wide, axis=1)
    (stat_g,) = staged_gather(
        [jnp.broadcast_to(stat_own[None], (8, token_rows))], [feat_dims], 7, span
    )
    stat_one = jnp.sum(stat_g[:, 0], axis=0)[:, None]
    grad_inputs = (
        d_attn.astype(f32)
        + scale_one * attn_gain[None, :] * back_one
        - inputs_wide * scale_one**3 * stat_one / MODEL_WIDTH
    )
    gain_one_term = jnp.sum(back_one * inputs_wide * scale_one, axis=0)

    def split_columns(a):
        return a.reshape(a.shape[0], tok_count, -1)

    qkv_term = jnp.concatenate(
        [
            split_columns(projection_gradient[:, :query_width]),
            split_columns(projection_gradient[:, query_width : query_width + kv_width]),
            split_columns(projection_gradient[:, query_width + kv_width :]),
        ],
        axis=2,
    ).transpose(1, 0, 2)
    rows_term = jnp.concatenate(
        [
            grad_out.reshape(tok_count, out_rows, own_width),
            jnp.broadcast_to(
                jnp.stack([gain_one_term, gain_two_term])[None], (tok_count, 2, own_width)
            ),
            jnp.zeros((tok_count, padded_rows - out_rows - 2, own_width), f32),
        ],
        axis=1,
    )
    rows_sum, qkv_sum = staged_reduce(
        [rows_term.astype(bf16), qkv_term.astype(bf16)],
        [("y", "k")] * 2,
        8,
        span,
    )
    ffn_sum = sum(part.astype(f32) for part in ffn_parts)
    return (
        block_out.T,
        grad_inputs.T,
        rows_sum[out_rows],
        qkv_sum[:, :q_part],
        qkv_sum[:, q_part : q_part + k_part],
        qkv_sum[:, q_part + k_part :],
        rows_sum[:out_rows],
        rows_sum[out_rows + 1],
        ffn_sum[:, :ff_own],
        ffn_sum[:, ff_own : 2 * ff_own],
        ffn_sum[:, 2 * ff_own :].T,
    )


def solution(mesh):
    return jax.shard_map(
        on_device,
        mesh=mesh,
        in_specs=(
            P("tok", "feat"),
            P("feat"),
            P("feat", "tok"),
            P("feat", "tok"),
            P("feat", "tok"),
            P("tok", "feat"),
            P("feat"),
            P("tok", "feat"),
            P("tok", "feat"),
            P("feat", "tok"),
            P("tok", "feat"),
        ),
        out_specs=(
            P("feat", "tok"),
            P("feat", "tok"),
            P("feat"),
            P("feat", "tok"),
            P("feat", "tok"),
            P("feat", "tok"),
            P("tok", "feat"),
            P("feat"),
            P("tok", "feat"),
            P("tok", "feat"),
            P("feat", "tok"),
        ),
        check_vma=False,
    )
```

```python
import itertools
import math

import jax
import jax.numpy as jnp
from jax import lax
from jax.experimental import pallas as pl
from jax.experimental.pallas import tpu as pltpu
from jax.sharding import PartitionSpec as P

MODEL_WIDTH = 960
QUERY_HEADS = 15
KEY_HEADS = 5
HEAD_SIZE = 64
SEQ_LEN = 4096
QUERY_PER_KEY = 3


EPS = 1e-05
ROPE_BASE = 10000.0
LARGE_NEGATIVE = -1e30


def rotary_tables(positions):
    half_width = HEAD_SIZE // 2
    inverse_freq = ROPE_BASE ** (-2.0 * jnp.arange(half_width, dtype=jnp.float32) / HEAD_SIZE)
    angles = positions.astype(jnp.float32)[:, None] * inverse_freq[None, :]
    return (jnp.cos(angles)[:, None, :], jnp.sin(angles)[:, None, :])


def apply_rotary(value_matrix, cosine_lookup, sine_lookup, head_count, sign_value):
    shaped = value_matrix.reshape(value_matrix.shape[0], head_count, HEAD_SIZE)
    lead_half = shaped[..., : HEAD_SIZE // 2]
    tail_half = shaped[..., HEAD_SIZE // 2 :]
    out_lead = lead_half * cosine_lookup - sign_value * tail_half * sine_lookup
    out_tail = tail_half * cosine_lookup + sign_value * lead_half * sine_lookup
    return jnp.concatenate([out_lead, out_tail], axis=-1).reshape(
        value_matrix.shape[0], head_count * HEAD_SIZE
    )


def divide_pair(value_matrix):
    high = value_matrix.astype(jnp.bfloat16)
    high = lax.optimization_barrier(high)
    low = (value_matrix - high.astype(jnp.float32)).astype(jnp.bfloat16)
    return high.astype(jnp.float32) + low.astype(jnp.float32)


VMEM_LIMIT = 56 * 1024 * 1024


class Place:
    def __init__(self, span):
        self.tok = lax.axis_index("tok")
        self.feat = lax.axis_index("feat")
        self.span = span
        tok_count, feat_count = lax.axis_size("tok"), lax.axis_size("feat")
        self.sizes = {"k": tok_count // 2, "ks": span // 2, "y": 2, "x": feat_count // 2, "c": 2}
        within = lax.rem(self.tok, span)
        self.base = self.tok - within
        self.at = {
            "k": lax.div(self.tok, 2),
            "ks": lax.div(within, 2),
            "y": lax.rem(self.tok, 2),
            "x": lax.div(self.feat, 2),
            "c": lax.rem(self.feat, 2),
        }

    def moved(self, dim, step):
        return lax.rem(self.at[dim] + step, self.sizes[dim])

    def index(self, offsets):
        result = 0
        for dim in ("k", "ks", "y", "x", "c"):
            if dim in offsets:
                result = result * self.sizes[dim] + self.moved(dim, offsets[dim])
        return result

    def peer(self, dim, step):
        tok, feat = self.tok, self.feat
        value = self.moved(dim, step)
        if dim == "k":
            tok = value * 2 + self.at["y"]
        elif dim == "ks":
            tok = self.base + value * 2 + self.at["y"]
        elif dim == "y":
            tok = self.at["k"] * 2 + value
        elif dim == "x":
            feat = value * 2 + self.at["c"]
        else:
            feat = self.at["x"] * 2 + value
        return {"tok": tok, "feat": feat}


def greet(place, dims):
    barrier = pltpu.get_barrier_semaphore()
    count = 0
    for dim in dims:
        for step in range(1, place.sizes[dim]):
            pl.semaphore_signal(
                barrier,
                inc=1,
                device_id=place.peer(dim, step),
                device_id_type=pl.DeviceIdType.MESH,
            )
            count += 1
    pl.semaphore_wait(barrier, count)


def all_dims(jobs):
    return [dim for dim in ("k", "ks", "y", "x", "c") if any(dim in job for job in jobs)]


def dim_sizes(span):
    return {
        "k": lax.axis_size("tok") // 2,
        "ks": span // 2,
        "y": 2,
        "x": lax.axis_size("feat") // 2,
        "c": 2,
    }


def staged_gather(arrays, jobs, collective, span):
    sizes = dim_sizes(span)
    count = len(arrays)
    slots = {}
    for j, dims in enumerate(jobs):
        for s, dim in enumerate(dims):
            for held in itertools.product(*[range(sizes[d]) for d in dims[:s]]):
                for step in range(1, sizes[dim]):
                    slots[j, s, held, step] = len(slots)
    totals = [math.prod(sizes[d] for d in dims) for dims in jobs]

    def kernel(*refs):
        ins, outs = refs[:count], refs[count : 2 * count]
        send_sem, recv_sem, local_sem = refs[2 * count :]
        place = Place(span)
        greet(place, all_dims(jobs))

        def block(j, held):
            dims = jobs[j]
            offsets = dict(zip(dims, tuple(held) + (0,) * (len(dims) - len(held))))
            return outs[j].at[place.index(offsets)]

        def copy(j, s, held, step, src, dst):
            slot = slots[j, s, held, step]
            return pltpu.make_async_remote_copy(
                src_ref=src,
                dst_ref=dst,
                send_sem=send_sem.at[slot],
                recv_sem=recv_sem.at[slot],
                device_id=place.peer(jobs[j][s], step),
                device_id_type=pl.DeviceIdType.MESH,
            )

        sent = []

        def forward(j, held, first, src):
            dims = jobs[j]
            for s in range(first, len(dims)):
                padded = held + (0,) * (s - len(held))
                for step in range(1, sizes[dims[s]]):
                    moving = copy(j, s, padded, step, src, block(j, padded))
                    moving.start()
                    sent.append(moving)

        local = []
        for j in range(count):
            forward(j, (), 0, ins[j])
            own = pltpu.make_async_copy(ins[j], block(j, ()), local_sem.at[j])
            own.start()
            local.append(own)
        for s in range(max(len(dims) for dims in jobs)):
            for j, dims in enumerate(jobs):
                if s >= len(dims):
                    continue
                size = sizes[dims[s]]
                for held in itertools.product(*[range(sizes[d]) for d in dims[:s]]):
                    for step in range(1, size):
                        arrived = held + ((size - step) % size,)
                        landed = block(j, arrived)
                        copy(j, s, held, step, landed, landed).wait_recv()
                        forward(j, arrived, s + 1, landed)
        for moving in sent:
            moving.wait_send()
        for own in local:
            own.wait()

    return pl.pallas_call(
        kernel,
        out_shape=[
            jax.ShapeDtypeStruct((total,) + a.shape, a.dtype) for total, a in zip(totals, arrays)
        ],
        in_specs=[pl.BlockSpec(memory_space=pl.ANY)] * count,
        out_specs=[pl.BlockSpec(memory_space=pl.ANY)] * count,
        scratch_shapes=[
            pltpu.SemaphoreType.DMA((len(slots),)),
            pltpu.SemaphoreType.DMA((len(slots),)),
            pltpu.SemaphoreType.DMA((count,)),
        ],
        compiler_params=pltpu.CompilerParams(collective_id=collective, has_side_effects=True),
    )(*arrays)


def staged_reduce(arrays, jobs, collective, span):
    sizes = dim_sizes(span)
    count = len(arrays)
    slots, scratch, where = {}, [], {}
    for j, dims in enumerate(jobs):
        tile = arrays[j].shape[1:]
        for s in range(len(dims)):
            rest = math.prod(sizes[d] for d in dims[s + 1 :])
            for step in range(1, sizes[dims[s]]):
                for held in itertools.product(*[range(sizes[d]) for d in dims[s + 1 :]]):
                    slots[j, s, step, held] = len(slots)
            where["recv", j, s] = len(scratch)
            scratch.append(pltpu.VMEM(((sizes[dims[s]] - 1) * rest,) + tile, jnp.bfloat16))
            if s < len(dims) - 1:
                where["sum", j, s] = len(scratch)
                scratch.append(pltpu.VMEM((rest,) + tile, jnp.bfloat16))

    def flat(dims, held):
        result = 0
        for d, offset in zip(dims, held):
            result = result * sizes[d] + offset
        return result

    def kernel(*refs):
        ins, outs = refs[:count], refs[count : 2 * count]
        buffers = refs[2 * count : 2 * count + len(scratch)]
        send_sem, recv_sem = refs[2 * count + len(scratch) :]
        place = Place(span)
        greet(place, all_dims(jobs))

        def source(j, s, held):
            dims = jobs[j]
            if s == 0:
                return ins[j].at[place.index(dict(zip(dims, held)))]
            return buffers[where["sum", j, s - 1]].at[flat(dims[s:], held)]

        def landing(j, s, step, held):
            dims = jobs[j]
            rest = math.prod(sizes[d] for d in dims[s + 1 :])
            return buffers[where["recv", j, s]].at[(step - 1) * rest + flat(dims[s + 1 :], held)]

        def copy(j, s, step, held):
            slot = slots[j, s, step, held]
            return pltpu.make_async_remote_copy(
                src_ref=source(j, s, (step,) + held),
                dst_ref=landing(j, s, step, held),
                send_sem=send_sem.at[slot],
                recv_sem=recv_sem.at[slot],
                device_id=place.peer(jobs[j][s], step),
                device_id_type=pl.DeviceIdType.MESH,
            )

        sent = []

        def start(j, s, step, held):
            moving = copy(j, s, step, held)
            moving.start()
            sent.append(moving)

        def offsets_of(dims):
            return reversed(list(itertools.product(*[range(sizes[d]) for d in dims])))

        for j, dims in enumerate(jobs):
            for held in offsets_of(dims[1:]):
                for step in range(1, sizes[dims[0]]):
                    start(j, 0, step, held)
        for s in range(max(len(dims) for dims in jobs)):
            for j, dims in enumerate(jobs):
                if s >= len(dims):
                    continue
                last = s == len(dims) - 1
                for held in offsets_of(dims[s + 1 :]):
                    steps = range(1, sizes[dims[s]])
                    for step in steps:
                        copy(j, s, step, held).wait_recv()
                    own = source(j, s, (0,) + held)
                    parts = [landing(j, s, step, held) for step in steps]
                    into = outs[j] if last else buffers[where["sum", j, s]].at[flat(dims[s + 1 :], held)]

                    @pl.loop(0, arrays[j].shape[1] // 16)
                    def _(chunk):
                        rows = pl.ds(pl.multiple_of(chunk * 16, 16), 16)
                        total = own[rows, :].astype(jnp.float32)
                        for part in parts:
                            total = total + part[rows, :].astype(jnp.float32)
                        into[rows, :] = total.astype(into.dtype)

                    if not last and held[0] != 0:
                        start(j, s + 1, held[0], held[1:])
        for moving in sent:
            moving.wait_send()

    return pl.pallas_call(
        kernel,
        out_shape=[jax.ShapeDtypeStruct(a.shape[1:], jnp.float32) for a in arrays],
        in_specs=[pl.BlockSpec(memory_space=pltpu.VMEM)] * count,
        out_specs=[pl.BlockSpec(memory_space=pltpu.VMEM)] * count,
        scratch_shapes=scratch
        + [pltpu.SemaphoreType.DMA((len(slots),)), pltpu.SemaphoreType.DMA((len(slots),))],
        compiler_params=pltpu.CompilerParams(
            collective_id=collective, has_side_effects=True, vmem_limit_bytes=VMEM_LIMIT
        ),
    )(*arrays)


def moved_along(value, axis, step):
    count = lax.axis_size(axis)
    return lax.ppermute(value, axis, [(i, (i + step) % count) for i in range(count)])


def placed_along(parts, axis):
    count = lax.axis_size(axis)
    index = lax.axis_index(axis)
    result = jnp.zeros((count,) + parts[0].shape, parts[0].dtype)
    for step, part in enumerate(parts):
        result = lax.dynamic_update_index_in_dim(
            result, part, lax.rem(index + count - step, count), 0
        )
    return result


def exchanged_along(blocks, axis):
    count = lax.axis_size(axis)
    index = lax.axis_index(axis)

    def picked(step):
        return lax.dynamic_index_in_dim(blocks, lax.rem(index + step, count), 0, keepdims=False)

    return [picked(0)] + [moved_along(picked(step), axis, step) for step in range(1, count)]


def on_device(
    inputs, attn_gain, w_query, w_key, value_weight, w_out, ffn_gain, w_gate, w_up, w_down, cot
):
    f32, bf16 = jnp.float32, jnp.bfloat16
    token_rows, own_width = inputs.shape
    feat_count = lax.axis_size("feat")
    tok_count = lax.axis_size("tok")
    local_rows = token_rows // feat_count
    span = SEQ_LEN // token_rows
    query_width = QUERY_HEADS * HEAD_SIZE
    kv_width = KEY_HEADS * HEAD_SIZE
    qkv_width = query_width + 2 * kv_width
    score_scale = 1.0 / math.sqrt(HEAD_SIZE)
    feat_index = lax.axis_index("feat")
    depth = lax.rem(lax.axis_index("tok"), span)
    own_first = feat_index * local_rows
    rows = depth * token_rows + own_first + jnp.arange(local_rows, dtype=jnp.int32)
    cosine_lookup, sine_lookup = rotary_tables(rows)
    ff_own = w_gate.shape[1]
    out_rows = w_out.shape[0]
    padded_rows = -(-(out_rows + 2) // 16) * 16

    def padded(a):
        return jnp.pad(a, ((0, padded_rows - out_rows), (0, 0)))

    tok_dims, feat_dims = ("k", "y"), ("x", "c")
    qkv_shards, inputs_g, wo_shards, cot_g, gains_g = staged_gather(
        [
            jnp.concatenate([w_query, w_key, value_weight], axis=1),
            inputs,
            padded(w_out),
            cot,
            jnp.broadcast_to(ffn_gain[None], (8, own_width)),
        ],
        [tok_dims, feat_dims, tok_dims + feat_dims, feat_dims, feat_dims],
        0,
        span,
    )
    ffn_shard = jnp.concatenate([w_gate, w_up, w_down.T], axis=1)
    ffn_shard, qkv_shards = lax.optimization_barrier((ffn_shard, qkv_shards))
    ffn_shards = [ffn_shard] + [
        moved_along(ffn_shard, "tok", step) for step in range(1, tok_count)
    ]
    early = -(-5 * tok_count // 8) + 1
    q_part, k_part = w_query.shape[1], w_key.shape[1]
    shard_columns = qkv_shards.transpose(1, 0, 2)
    qkv_weights = jnp.concatenate(
        [
            shard_columns[:, :, :q_part].reshape(own_width, query_width),
            shard_columns[:, :, q_part : q_part + k_part].reshape(own_width, kv_width),
            shard_columns[:, :, q_part + k_part :].reshape(own_width, kv_width),
        ],
        axis=1,
    )
    inputs_all = inputs_g.transpose(1, 0, 2).reshape(token_rows, MODEL_WIDTH)
    cot_all = cot_g.transpose(1, 0, 2).reshape(token_rows, MODEL_WIDTH)
    gain_all = gains_g[:, 0].reshape(MODEL_WIDTH)
    wo_all = (
        wo_shards.reshape(tok_count, feat_count, padded_rows, own_width)[:, :, :out_rows]
        .transpose(0, 2, 1, 3)
        .reshape(query_width, MODEL_WIDTH)
    )

    inputs_all_wide = inputs_all.astype(f32)
    inputs_wide = inputs.astype(f32)
    scale_one = lax.rsqrt(jnp.mean(inputs_all_wide * inputs_all_wide, axis=1, keepdims=True) + EPS)
    normed_one = (inputs_wide * scale_one * attn_gain[None, :]).astype(bf16)
    (projection,) = staged_reduce(
        [
            jnp.dot(normed_one, qkv_weights, preferred_element_type=f32)
            .astype(bf16)
            .reshape(feat_count, local_rows, qkv_width)
        ],
        [("c", "x")],
        1,
        span,
    )
    queries = apply_rotary(
        projection[:, :query_width], cosine_lookup, sine_lookup, QUERY_HEADS, 1.0
    ).astype(bf16)
    keys = apply_rotary(
        projection[:, query_width : query_width + kv_width],
        cosine_lookup,
        sine_lookup,
        KEY_HEADS,
        1.0,
    ).astype(bf16)
    values = projection[:, query_width + kv_width :].astype(bf16)
    kv_own = jnp.concatenate([keys, values], axis=1)
    cut = min(-(-kv_width // 128) * 128, 2 * kv_width)
    kv_first, kv_second = staged_gather(
        [kv_own[:, :cut], kv_own[:, cut:]],
        [("ks", "y", "x", "c"), ("ks", "x", "y", "c")],
        2,
        span,
    )
    kv_blocks = jnp.concatenate([kv_first, kv_second], axis=2).reshape(
        span, token_rows, 2 * kv_width
    )
    kv_blocks, ffn_shards[:early] = lax.optimization_barrier((kv_blocks, ffn_shards[:early]))
    query_rows = queries.reshape(local_rows, KEY_HEADS, QUERY_PER_KEY, HEAD_SIZE).transpose(
        1, 2, 0, 3
    )

    def block_of(turn):
        piece = lax.dynamic_index_in_dim(kv_blocks, turn, 0, keepdims=False)
        return (
            piece[:, :kv_width].reshape(token_rows, KEY_HEADS, HEAD_SIZE),
            piece[:, kv_width:].reshape(token_rows, KEY_HEADS, HEAD_SIZE),
        )

    def allowed_of(turn):
        key_pos = turn * token_rows + jnp.arange(token_rows, dtype=jnp.int32)
        return key_pos[None, :] <= rows[:, None]

    def attend(turn, carried):
        maxima, totals, weighted = carried
        key_set, value_set = block_of(turn)
        scores = (
            jnp.einsum("gcrd,ngd->gcrn", query_rows, key_set, preferred_element_type=f32)
            * score_scale
        )
        masked = jnp.where(allowed_of(turn), scores, LARGE_NEGATIVE)
        new_max = jnp.maximum(maxima, jnp.max(masked, axis=-1))
        weights = jnp.exp(masked - new_max[..., None])
        factor = jnp.exp(maxima - new_max)
        return (
            new_max,
            totals * factor + jnp.sum(weights, axis=-1),
            weighted * factor[..., None]
            + jnp.einsum(
                "gcrn,ngd->gcrd", weights.astype(bf16), value_set, preferred_element_type=f32
            ),
        )

    state = (KEY_HEADS, QUERY_PER_KEY, local_rows)
    maxima, totals, weighted = lax.fori_loop(
        0,
        depth + 1,
        attend,
        (
            jnp.full(state, LARGE_NEGATIVE, f32),
            jnp.zeros(state, f32),
            jnp.zeros(state + (HEAD_SIZE,), f32),
        ),
    )
    heads_rows = (weighted / totals[..., None]).astype(bf16)
    heads_out = heads_rows.transpose(2, 0, 1, 3).reshape(local_rows, query_width)
    log_used = divide_pair(maxima + jnp.log(totals))
    (heads_g,) = staged_gather([heads_out], [feat_dims], 3, span)
    heads_all = heads_g.reshape(token_rows, query_width)

    ffn_weights = placed_along(ffn_shards, "tok").reshape(MODEL_WIDTH, 3 * ff_own)
    gate_up, down_turned = ffn_weights[:, : 2 * ff_own], ffn_weights[:, 2 * ff_own :]
    residual_all = inputs_all_wide + jnp.dot(heads_all, wo_all, preferred_element_type=f32)
    scale_two = lax.rsqrt(jnp.mean(residual_all * residual_all, axis=1, keepdims=True) + EPS)
    normed_two = (residual_all * scale_two * gain_all[None, :]).astype(bf16)
    gate_up_pre = jnp.dot(normed_two, gate_up, preferred_element_type=f32)
    gate_pre, up_pre = gate_up_pre[:, :ff_own], gate_up_pre[:, ff_own:]
    sigmoid_gate = jax.nn.sigmoid(gate_pre)
    hidden = (gate_pre * sigmoid_gate * up_pre).astype(bf16)
    ffn_partial = jnp.dot(hidden, down_turned.T, preferred_element_type=f32).astype(bf16)
    d_hidden = jnp.dot(cot_all, down_turned, preferred_element_type=f32)
    d_gate = (d_hidden * up_pre * sigmoid_gate * (1.0 + gate_pre * (1.0 - sigmoid_gate))).astype(
        bf16
    )
    d_up = (d_hidden * gate_pre * sigmoid_gate).astype(bf16)
    d_gate_up = jnp.concatenate([d_gate, d_up], axis=1)
    ffn_gradient = jnp.concatenate(
        [
            jnp.dot(normed_two.T, d_gate_up, preferred_element_type=f32).astype(bf16),
            jnp.dot(cot_all.T, hidden, preferred_element_type=f32).astype(bf16),
        ],
        axis=1,
    ).reshape(tok_count, out_rows, 3 * ff_own)
    ffn_parts = exchanged_along(ffn_gradient, "tok")
    back_two = jnp.dot(d_gate_up, gate_up.T, preferred_element_type=f32).astype(bf16)
    d_norm_two, ffn_term = staged_reduce(
        [
            back_two.reshape(feat_count, local_rows, MODEL_WIDTH),
            ffn_partial.reshape(token_rows, feat_count, own_width).transpose(1, 0, 2),
        ],
        [("c", "x"), ("c", "x")],
        4,
        span,
    )
    residual_own = lax.dynamic_slice_in_dim(
        residual_all, feat_index * own_width, own_width, 1
    )
    block_out = residual_own + ffn_term

    def own_rows(a):
        return lax.dynamic_slice_in_dim(a, own_first, local_rows, 0)

    residual_rows, scale_rows = own_rows(residual_all), own_rows(scale_two)
    stat_two = jnp.sum(d_norm_two * gain_all[None, :] * residual_rows, axis=1, keepdims=True)
    d_mid_rows = (
        own_rows(cot_all).astype(f32)
        + scale_rows * gain_all[None, :] * d_norm_two
        - residual_rows * scale_rows**3 * stat_two / MODEL_WIDTH
    ).astype(bf16)
    gain_two_rows = jnp.sum(d_norm_two * residual_rows * scale_rows, axis=0)
    head_gradient = (
        jnp.dot(d_mid_rows, wo_all.T, preferred_element_type=f32)
        .astype(bf16)
        .reshape(local_rows, KEY_HEADS, QUERY_PER_KEY, HEAD_SIZE)
        .transpose(1, 2, 0, 3)
    )
    delta_used = divide_pair(
        jnp.sum(head_gradient.astype(f32) * heads_rows.astype(f32), axis=-1)
    )

    def backprop(turn, carried):
        query_sum, gradients = carried
        key_set, value_set = block_of(turn)
        scores = (
            jnp.einsum("gcrd,ngd->gcrn", query_rows, key_set, preferred_element_type=f32)
            * score_scale
        )
        masked = jnp.where(allowed_of(turn), scores, LARGE_NEGATIVE)
        probability = jnp.exp(masked - log_used[..., None])
        d_probs = jnp.einsum(
            "gcrd,ngd->gcrn", head_gradient, value_set, preferred_element_type=f32
        )
        d_scores = (probability * (d_probs - delta_used[..., None])).astype(bf16)
        query_sum = (
            query_sum
            + jnp.einsum("gcrn,ngd->gcrd", d_scores, key_set, preferred_element_type=f32)
            * score_scale
        )
        key_part = (
            jnp.einsum("gcrn,gcrd->ngd", d_scores, query_rows, preferred_element_type=f32)
            * score_scale
        )
        value_part = jnp.einsum(
            "gcrn,gcrd->ngd",
            probability.astype(bf16),
            head_gradient,
            preferred_element_type=f32,
        )
        part = jnp.concatenate(
            [key_part.reshape(token_rows, kv_width), value_part.reshape(token_rows, kv_width)],
            axis=1,
        ).astype(bf16)
        return (query_sum, lax.dynamic_update_index_in_dim(gradients, part, turn, 0))

    query_sum, gradients = lax.fori_loop(
        0,
        depth + 1,
        backprop,
        (
            jnp.zeros(state + (HEAD_SIZE,), f32),
            jnp.zeros((span, token_rows, 2 * kv_width), bf16),
        ),
    )
    gradients, ffn_parts[:early] = lax.optimization_barrier((gradients, ffn_parts[:early]))
    gradients = gradients.reshape(span * feat_count, local_rows, 2 * kv_width)
    kv_gradient = jnp.concatenate(
        staged_reduce(
            [gradients[:, :, :cut], gradients[:, :, cut:]],
            [("c", "x", "y", "ks"), ("c", "y", "x", "ks")],
            5,
            span,
        ),
        axis=1,
    )
    d_qkv_rows = jnp.concatenate(
        [
            apply_rotary(
                query_sum.transpose(2, 0, 1, 3).reshape(local_rows, query_width),
                cosine_lookup,
                sine_lookup,
                QUERY_HEADS,
                -1.0,
            ),
            apply_rotary(
                kv_gradient[:, :kv_width], cosine_lookup, sine_lookup, KEY_HEADS, -1.0
            ),
            kv_gradient[:, kv_width:],
        ],
        axis=1,
    ).astype(bf16)
    d_qkv_rows, ffn_parts[early:] = lax.optimization_barrier((d_qkv_rows, ffn_parts[early:]))
    d_qkv_g, d_mid_g, gain_two_g = staged_gather(
        [d_qkv_rows, d_mid_rows, jnp.broadcast_to(gain_two_rows[None], (8, MODEL_WIDTH))],
        [feat_dims, feat_dims, feat_dims],
        6,
        span,
    )
    d_qkv_all = d_qkv_g.reshape(token_rows, qkv_width)
    d_attn = lax.dynamic_slice_in_dim(
        d_mid_g.reshape(token_rows, MODEL_WIDTH), feat_index * own_width, own_width, 1
    )
    gain_two_term = lax.dynamic_slice_in_dim(
        jnp.sum(gain_two_g[:, 0], axis=0), feat_index * own_width, own_width, 0
    )
    grad_out = jnp.dot(heads_all.T, d_attn, preferred_element_type=f32)
    projection_gradient = jnp.dot(normed_one.T, d_qkv_all, preferred_element_type=f32)
    back_one = jnp.dot(d_qkv_all, qkv_weights.T, preferred_element_type=f32)
    stat_own = jnp.sum(back_one * attn_gain[None, :] * inputs_wide, axis=1)
    (stat_g,) = staged_gather(
        [jnp.broadcast_to(stat_own[None], (8, token_rows))], [feat_dims], 7, span
    )
    stat_one = jnp.sum(stat_g[:, 0], axis=0)[:, None]
    grad_inputs = (
        d_attn.astype(f32)
        + scale_one * attn_gain[None, :] * back_one
        - inputs_wide * scale_one**3 * stat_one / MODEL_WIDTH
    )
    gain_one_term = jnp.sum(back_one * inputs_wide * scale_one, axis=0)

    def split_columns(a):
        return a.reshape(a.shape[0], tok_count, -1)

    qkv_term = jnp.concatenate(
        [
            split_columns(projection_gradient[:, :query_width]),
            split_columns(projection_gradient[:, query_width : query_width + kv_width]),
            split_columns(projection_gradient[:, query_width + kv_width :]),
        ],
        axis=2,
    ).transpose(1, 0, 2)
    rows_term = jnp.concatenate(
        [
            grad_out.reshape(tok_count, out_rows, own_width),
            jnp.broadcast_to(
                jnp.stack([gain_one_term, gain_two_term])[None], (tok_count, 2, own_width)
            ),
            jnp.zeros((tok_count, padded_rows - out_rows - 2, own_width), f32),
        ],
        axis=1,
    )
    rows_sum, qkv_sum = staged_reduce(
        [rows_term.astype(bf16), qkv_term.astype(bf16)],
        [("y", "k")] * 2,
        8,
        span,
    )
    ffn_sum = sum(part.astype(f32) for part in ffn_parts)
    return (
        block_out.T,
        grad_inputs.T,
        rows_sum[out_rows],
        qkv_sum[:, :q_part],
        qkv_sum[:, q_part : q_part + k_part],
        qkv_sum[:, q_part + k_part :],
        rows_sum[:out_rows],
        rows_sum[out_rows + 1],
        ffn_sum[:, :ff_own],
        ffn_sum[:, ff_own : 2 * ff_own],
        ffn_sum[:, 2 * ff_own :].T,
    )


def solution(mesh):
    return jax.shard_map(
        on_device,
        mesh=mesh,
        in_specs=(
            P("tok", "feat"),
            P("feat"),
            P("feat", "tok"),
            P("feat", "tok"),
            P("feat", "tok"),
            P("tok", "feat"),
            P("feat"),
            P("tok", "feat"),
            P("tok", "feat"),
            P("feat", "tok"),
            P("tok", "feat"),
        ),
        out_specs=(
            P("feat", "tok"),
            P("feat", "tok"),
            P("feat"),
            P("feat", "tok"),
            P("feat", "tok"),
            P("feat", "tok"),
            P("tok", "feat"),
            P("feat"),
            P("tok", "feat"),
            P("tok", "feat"),
            P("feat", "tok"),
        ),
        check_vma=False,
    )
```
